256 devices in a mesh: pipe: 8 (over z_hi, x), edp: 32 (over y, z_lo, core).
Axes of the slice: x: 4, y: 4, z: 8 (z_hi: 2, z_lo: 4; z = z_hi * 4 + z_lo), core: 2. Of those that a mesh axis runs over, the one named last changes fastest.
Arguments:
- hidden_act: bfloat16 [65536, 1024], P(('pipe', 'edp')), may hold values from -24 to 24
- grad_out: bfloat16 [65536, 7168], P(('pipe', 'edp')), may hold values from -0.08984375 to 0.08984375
- live_tokens: int32 [8, 32], replicated, may hold values from 1 to 256, 2730 in all within a row
- block_count: int32 [8, 32], replicated, may hold values from 1 to 4, 64 in all within a row
- master: float32 [8, 1024, 7168], P('pipe', 'edp'), may hold values from -6 to 6
- moment1: bfloat16 [8, 1024, 7168], P('pipe', 'edp'), may hold values from -1.796875 to 1.796875
- moment2: bfloat16 [8, 1024, 7168], P('pipe', 'edp'), may hold values from 0.0099487305 to 1
Outputs:
- new_master: float32 [8, 1024, 7168], P('pipe', 'edp')
- new_first: bfloat16 [8, 1024, 7168], P('pipe', 'edp')
- new_second: bfloat16 [8, 1024, 7168], P('pipe', 'edp')
The draws below stay inside these ranges and needn't reach their ends.
Inputs may be any that keep to these rules, and one draw needn't show every extreme that they name: live_tokens[p, e] counts the leading token slots of device (p, e) that hold routed tokens. Each row sums to 2730, and its largest entry is exactly 256. block_count[p, o] is the number of consecutive blocks of rank p's half that owner o holds, owners in order. Each row sums to 64, and its largest entry is exactly 4.
All inputs are finite; a program needn't handle non-finite values.
Results may differ from the reference program's by a relative error of at most 0.0085.
Values may be sent and summed in bfloat16 or wider, within the bound.
No kernel may reach another device: no remote copies, remote signals or barrier semaphores. Data moves between devices by JAX's collectives and lax.ppermute only.
A program may use at most 128 MiB of HBM per device.

```python
import math
import jax
import jax.numpy as jnp
import numpy as np
from jax import lax

D = 7168
HID = 1024
BLK = 8
TOK_DEV = 256
TOKENS = 65536
HBLK = 64
CAP = 4
SLOTS = 32
N_PIPE = 8
N_EDP = 32


def strengthened(values, own_key, source, target, shards_of, factor):
    owner, partner = [(jnp.arange(values.shape[axis_at]) // (values.shape[axis_at] // shards_of)).reshape([-1 if axis == axis_at else 1 for axis in range(values.ndim)]) for axis_at in (source, target)]
    chosen = jax.random.permutation(own_key, shards_of)[partner]
    strong = (owner == chosen) | (owner == (partner + shards_of // 2) % shards_of)
    return jnp.where(strong, factor * values, values)


def steps_of(rng, dims, cuts, smallest, largest):
    gain, own = 1.0, jax.random.fold_in(rng, 6)
    for dim, blocks in cuts:
        heights = jnp.exp(jax.random.uniform(jax.random.fold_in(own, dim), (blocks,), jnp.float32, smallest / len(cuts), largest / len(cuts)))
        gain = gain * jnp.repeat(heights, dims[dim] // blocks).reshape([-1 if axis == dim else 1 for axis in range(len(dims))])
    return gain


def split_up(count, total, bound, skew):
    portions = [(1 << 20) // math.isqrt(standing ** skew) + 1 for standing in range(2, count + 1)]
    spare, holding = total - bound - (count - 1), [1] * (count - 1)
    while spare > 0:
        free = [i for i in range(count - 1) if holding[i] < bound]
        pool, budget = sum([portions[i] for i in free]), spare
        for i in free:
            addition = min(bound - holding[i], max(1, budget * portions[i] // pool), spare)
            holding[i] = holding[i] + addition
            spare = spare - addition
    return np.array([bound] + holding)


def uneven(key, amount, total, limit, slope):
    if amount == 2:
        one = jax.random.randint(key, (), max(1, total - limit), min(limit, total - 1) + 1)
        return jnp.stack([one, total - one])
    sizes = jnp.asarray(split_up(amount, total, limit, slope), jnp.int32)
    twos = (amount - 1) // 2
    giver, receiver = sizes[1:1 + 2 * twos:2], sizes[2:2 + 2 * twos:2]
    slack = jnp.minimum(giver - 1, limit - receiver)
    shifted = jax.random.randint(jax.random.fold_in(key, 1), (twos,), 0, 1 << 20) % (slack + 1)
    sizes = sizes.at[1:1 + 2 * twos:2].set(giver - shifted).at[2:2 + 2 * twos:2].set(receiver + shifted)
    return sizes[jax.random.permutation(jax.random.fold_in(key, 2), amount)]


def centred(stream_key, dims, spread, limit, shards=(), kind=jnp.bfloat16):
    factor_of = steps_of(stream_key, dims, shards, -0.22, 0.18) if shards else 1.0
    result = jax.random.normal(stream_key, dims, jnp.float32) * spread * factor_of
    return jnp.minimum(jnp.maximum(result, -limit), limit).astype(kind)


def heavy_noise(stream_key, extent, spread, limit, cuts, heavy, kind=jnp.bfloat16):
    drawn = spread * jax.random.normal(stream_key, extent, jnp.float32)
    if cuts:
        drawn = drawn * steps_of(stream_key, extent, cuts, -0.22, 0.18)
    return jnp.clip(strengthened(drawn, jax.random.fold_in(stream_key, 3), *heavy), -limit, limit).astype(kind)


def setup_inputs(seed: int = 0) -> dict:
    key_list = jax.random.split(jax.random.key(seed), 8)
    return {
        "hidden_act": heavy_noise(key_list[0], (TOKENS, HID), 1.0, 24.0, ((0, 256),), (0, 1, 256, 6.0)),
        "grad_out": centred(key_list[1], (TOKENS, D), 0.015, 0.08984375, ((0, 256),)),
        "live_tokens": jax.vmap(lambda own: uneven(own, N_EDP, N_EDP * TOK_DEV // 3, TOK_DEV, 2))(jax.random.split(key_list[2], N_PIPE)).reshape((N_PIPE, N_EDP)).astype(jnp.int32),
        "block_count": jax.vmap(lambda own: uneven(own, N_EDP, HBLK, CAP, 2))(jax.random.split(key_list[3], N_PIPE)).reshape((N_PIPE, N_EDP)).astype(jnp.int32),
        "master": centred(key_list[4], (N_PIPE, N_EDP * SLOTS, D), 1.0, 6.0, ((0, 8), (1, 32)), jnp.float32),
        "moment1": centred(key_list[5], (N_PIPE, N_EDP * SLOTS, D), 0.3, 1.796875, ((0, 8), (1, 32))),
        "moment2": jnp.clip(jnp.exp(math.log(1.0) - 4.61031033 * jax.random.uniform(key_list[6], (N_PIPE, N_EDP * SLOTS, D), jnp.float32) ** steps_of(key_list[6], (N_PIPE, N_EDP * SLOTS, D), ((0, 8), (1, 32)), -0.2, 0.2)), 0.0099487305, 1.0).astype(jnp.bfloat16),
    }


beta_first = 0.9
beta_second = 0.95
learn_rate = 0.00022
weight_decay = 0.1
adam_eps = 1e-08
bias_first = 1.0 - 0.9 ** 20
bias_second = 1.0 - 0.95 ** 20

def adamw(param, first_old, second_old, owned_bf, valid):
    owned = owned_bf.astype(jnp.float32)
    first = beta_first * first_old.astype(jnp.float32) + (1.0 - beta_first) * owned
    second = beta_second * second_old.astype(jnp.float32) + (1.0 - beta_second) * owned * owned
    direction = first / bias_first / (jnp.sqrt(second / bias_second) + adam_eps)
    updated = param - learn_rate * (direction + weight_decay * param)
    zero_f = jnp.zeros((), jnp.float32)
    new_master = jnp.where(valid, updated, zero_f)
    new_first = jnp.where(valid, first, zero_f).astype(jnp.bfloat16)
    new_second = jnp.where(valid, second, zero_f).astype(jnp.bfloat16)
    return (new_master, new_first, new_second)

def pair_product(own_hidden, own_grad, far_hidden, far_grad):
    left = jnp.concatenate([own_hidden, far_hidden], 0)
    right = jnp.concatenate([own_grad, far_grad], 0)
    return lax.dot_general(left, right, (((0,), (0,)), ((), ())), preferred_element_type=jnp.float32)

def reference(hidden_act, grad_out, live_tokens, block_count, master, moment1, moment2):
    hid = hidden_act.reshape(N_PIPE, N_EDP, TOK_DEV, HID)
    grd = grad_out.reshape(N_PIPE, N_EDP, TOK_DEV, D)
    positions = jnp.arange(TOK_DEV, dtype=jnp.int32)
    half = HID // 2
    outs_master, outs_first, outs_second = ([], [], [])
    for prank in range(N_PIPE):
        mirror = N_PIPE - 1 - prank
        lower = half if prank >= N_PIPE // 2 else 0

        def add(total, erank):
            keep_a = (positions < live_tokens[prank, erank])[:, None]
            keep_b = (positions < live_tokens[mirror, erank])[:, None]
            zero_b = jnp.zeros((), grd.dtype)
            grad_a = jnp.where(keep_a, grd[prank, erank], zero_b)
            grad_b = jnp.where(keep_b, grd[mirror, erank], zero_b)
            part = pair_product(hid[prank, erank, :, lower:lower + half], grad_a, hid[mirror, erank, :, lower:lower + half], grad_b)
            part = lax.optimization_barrier(part.astype(jnp.bfloat16)).astype(jnp.float32)
            return (total + part, None)
        total, _ = lax.scan(add, jnp.zeros((half, D), jnp.float32), jnp.arange(N_EDP, dtype=jnp.int32))
        total_bf = lax.optimization_barrier(total.astype(jnp.bfloat16))
        counts = block_count[prank]
        starts = jnp.cumsum(counts) - counts
        slot = jnp.arange(CAP, dtype=jnp.int32)
        block_id = jnp.minimum(starts[:, None] + slot[None, :], HBLK - 1).astype(jnp.int32)
        valid = slot[None, :] < counts[:, None]
        blocks = total_bf.reshape(HBLK, BLK, D)
        picked = jnp.take(blocks, block_id, axis=0).reshape(N_EDP * SLOTS, D)
        valid_rows = jnp.broadcast_to(valid[:, :, None], (N_EDP, CAP, BLK)).reshape(N_EDP * SLOTS, 1)
        owned = jnp.where(valid_rows, picked, jnp.zeros((), jnp.bfloat16))
        new_master, new_first, new_second = adamw(master[prank], moment1[prank], moment2[prank], owned, valid_rows)
        outs_master.append(new_master)
        outs_first.append(new_first)
        outs_second.append(new_second)
    return (jnp.stack(outs_master), jnp.stack(outs_first), jnp.stack(outs_second))
```

```python
import functools
import jax
import jax.numpy as jnp
from jax import lax
from jax.experimental import pallas as pl
from jax.experimental.pallas import tpu as pltpu
from jax.sharding import Mesh, PartitionSpec as P

BLK = 8
CHUNKS = (256, 256, 384)
NY, NZ, NC = 4, 4, 2
OFFSETS = tuple((dy, dc) for dy in range(NY) for dc in range(NC))

beta_first = 0.9
beta_second = 0.95
learn_rate = 0.00022
weight_decay = 0.1
adam_eps = 1e-08
bias_first = 1.0 - 0.9**20
bias_second = 1.0 - 0.95**20

bf16 = jnp.bfloat16
f32 = jnp.float32
VMEM = pl.BlockSpec(memory_space=pltpu.VMEM)
SMEM = pl.BlockSpec(memory_space=pltpu.SMEM)
ANY = pl.BlockSpec(memory_space=pl.ANY)
PARAMS = pltpu.CompilerParams(vmem_limit_bytes=40 * 1024 * 1024)


def send_group(value, dy, dc):
    if dy == 0 and dc == 0:
        return value
    pairs = []
    for y in range(NY):
        for c in range(NC):
            pairs.append((y * NC + c, (y + dy) % NY * NC + (c ^ dc)))
    return lax.ppermute(value, ("y", "c"), pairs)


def send_ring(value):
    pairs = []
    for z in range(NZ):
        pairs.append((z, (z + 1) % NZ))
        pairs.append((NZ + z, NZ + (z + NZ - 1) % NZ))
    return lax.ppermute(value, ("zh", "z"), pairs)


def send_mirror(value):
    pairs = []
    for zh in range(2):
        for x in range(4):
            for z in range(NZ):
                source = (zh * 4 + x) * NZ + z
                target = ((1 - zh) * 4 + 3 - x) * NZ + NZ - 1 - z
                pairs.append((source, target))
    return lax.ppermute(value, ("zh", "x", "z"), pairs)


def ring_rank():
    z = lax.axis_index("z")
    return jnp.where(lax.axis_index("zh") == 0, z, NZ - 1 - z)


def prepare_kernel(live_ref, hidden_ref, out_ref):
    zh, x = lax.axis_index("zh"), lax.axis_index("x")
    y, z, c = lax.axis_index("y"), lax.axis_index("z"), lax.axis_index("c")
    live = live_ref[zh * 4 + x, (y * NZ + z) * NC + c]
    rank = jnp.where(zh == 0, z, NZ - 1 - z)
    rows = hidden_ref.shape[0]
    keep = lax.broadcasted_iota(jnp.int32, (128, rows), 1) < live
    for step in range(NZ):
        part = lax.rem(rank + 2 * NZ - 1 - step, NZ)
        for other in range(2):
            half = zh if other == 0 else 1 - zh
            block = (half * NZ + part) * 128
            cols = hidden_ref[:, pl.ds(pl.multiple_of(block, 128), 128)]
            turned = jnp.where(keep, cols.astype(f32).T, 0.0).astype(bf16)
            at = (step * 2 + other) * 128
            out_ref[at:at + 128, :] = turned


def prepare(hidden, live_tokens):
    return pl.pallas_call(
        prepare_kernel,
        out_shape=jax.ShapeDtypeStruct((hidden.shape[1], hidden.shape[0]), bf16),
        in_specs=[SMEM, VMEM],
        out_specs=VMEM,
        compiler_params=PARAMS,
        name="prepare",
    )(live_tokens, hidden)


def pack_kernel(grad_ref, *rest):
    out_refs, sem = rest[:-1], rest[-1]
    y, c = lax.axis_index("y"), lax.axis_index("c")
    width = sum(CHUNKS)
    copies = []
    for i, (dy, dc) in enumerate(OFFSETS):
        target = lax.rem(y + dy, NY) * NC + lax.rem(c + dc, NC)
        base = 0
        for k, cols in enumerate(CHUNKS):
            at = pl.multiple_of(target * width + base, 128)
            copy = pltpu.make_async_copy(
                grad_ref.at[:, pl.ds(at, cols)], out_refs[k * 8 + i], sem.at[k * 8 + i]
            )
            copy.start()
            copies.append(copy)
            base += cols
    for copy in copies:
        copy.wait()


def pack(grad):
    rows = grad.shape[0]
    shapes = [jax.ShapeDtypeStruct((rows, cols), bf16) for cols in CHUNKS for _ in OFFSETS]
    return pl.pallas_call(
        pack_kernel,
        out_shape=shapes,
        in_specs=[ANY],
        out_specs=[ANY] * len(shapes),
        scratch_shapes=[pltpu.SemaphoreType.DMA((len(shapes),))],
        compiler_params=PARAMS,
        name="pack",
    )(grad)


def product_kernel(*refs):
    hidden, grad, outs = refs[:8], refs[8:16], refs[16:]
    rows = outs[0].shape[0]
    for step, out_ref in enumerate(outs):
        total = None
        for h_ref, g_ref in zip(hidden, grad):
            term = jnp.dot(
                h_ref[step * rows:(step + 1) * rows, :], g_ref[...], preferred_element_type=f32
            )
            total = term if total is None else total + term
        out_ref[...] = total.astype(out_ref.dtype)


def product(hidden, grad):
    rows, cols = hidden[0].shape[0] // NZ, grad[0].shape[1]
    depth = sum(g.shape[0] for g in grad)
    shapes = [jax.ShapeDtypeStruct((rows, cols), bf16) for _ in range(NZ)]
    return pl.pallas_call(
        product_kernel,
        out_shape=shapes,
        in_specs=[VMEM] * 16,
        out_specs=[VMEM] * NZ,
        compiler_params=PARAMS,
        cost_estimate=pl.CostEstimate(
            flops=2 * rows * NZ * cols * depth,
            bytes_accessed=2 * (rows * NZ * (depth + cols) + depth * cols),
            transcendentals=0,
        ),
        name="product",
    )(*hidden, *grad)


def adamw_kernel(*refs):
    n = 8 * len(CHUNKS)
    counts_ref, owned_refs = refs[0], refs[1:1 + n]
    master_ref, first_ref, second_ref, new_master_ref, new_first_ref, new_second_ref = refs[1 + n:]
    zh, x = lax.axis_index("zh"), lax.axis_index("x")
    y, z, c = lax.axis_index("y"), lax.axis_index("z"), lax.axis_index("c")
    held = counts_ref[zh * 4 + x, (y * NZ + z) * NC + c]
    width = sum(CHUNKS)
    slots = master_ref.shape[0]
    for i, (dy, dc) in enumerate(OFFSETS):
        source = lax.rem(y + NY - dy, NY) * NC + lax.rem(c + dc, NC)
        base = 0
        for k, cols in enumerate(CHUNKS):
            at = pl.ds(pl.multiple_of(source * width + base, 128), cols)
            base += cols
            valid = lax.broadcasted_iota(jnp.int32, (slots, cols), 0) < held * BLK
            owned = owned_refs[k * 8 + i][...].astype(f32)
            param = master_ref[:, at]
            first = beta_first * first_ref[:, at].astype(f32) + (1.0 - beta_first) * owned
            second = beta_second * second_ref[:, at].astype(f32) + (1.0 - beta_second) * owned * owned
            direction = first / bias_first / (jnp.sqrt(second / bias_second) + adam_eps)
            updated = param - learn_rate * (direction + weight_decay * param)
            new_master_ref[:, at] = jnp.where(valid, updated, 0.0)
            new_first_ref[:, at] = jnp.where(valid, first, 0.0).astype(bf16)
            new_second_ref[:, at] = jnp.where(valid, second, 0.0).astype(bf16)


def adamw(block_count, owned, master, moment1, moment2):
    shapes = [jax.ShapeDtypeStruct(a.shape, a.dtype) for a in (master, moment1, moment2)]
    return pl.pallas_call(
        adamw_kernel,
        out_shape=shapes,
        in_specs=[SMEM] + [VMEM] * (len(owned) + 3),
        out_specs=[VMEM] * 3,
        compiler_params=PARAMS,
        name="adamw",
    )(block_count, *owned, master, moment1, moment2)


def slot_choice(block_count, hblk, cap):
    y, z, c = lax.axis_index("y"), lax.axis_index("z"), lax.axis_index("c")
    counts = block_count[lax.axis_index("zh") * 4 + lax.axis_index("x")]
    owners = []
    for dy, dc in OFFSETS:
        owners.append(((y + dy) % NY * NZ + z) * NC + (c ^ dc))
    owners = jnp.stack(owners)
    before = jnp.arange(counts.shape[0], dtype=jnp.int32)[None, :] < owners[:, None]
    starts = jnp.sum(jnp.where(before, counts[None, :], 0), axis=1)
    slot = jnp.arange(cap, dtype=jnp.int32)
    block = jnp.minimum(starts[:, None] + slot[None, :], hblk - 1)
    per = hblk // NZ
    place = (ring_rank() + NZ - block // per) % NZ * per + block % per
    rows = place[:, :, None] * BLK + jnp.arange(BLK, dtype=jnp.int32)
    rows = rows.reshape(-1)
    return (rows[:, None] == jnp.arange(hblk * BLK, dtype=jnp.int32)[None, :]).astype(bf16)


def per_device(hidden_act, grad_out, live_tokens, block_count, master, moment1, moment2):
    half = hidden_act.shape[1] // 2
    slots = master.shape[1]
    turned = prepare(hidden_act, live_tokens)
    same = [send_group(turned, dy, 0) for dy in range(NY)]
    hidden = []
    for value in same:
        hidden += [value, send_group(value, 0, 1)]
    packed = pack(grad_out)
    choice = slot_choice(block_count, half // BLK, slots // BLK)
    owned = []
    for k in range(len(CHUNKS)):
        grad = [send_group(packed[k * 8 + i], dy, dc) for i, (dy, dc) in enumerate(OFFSETS)]
        parts = product(hidden, grad)
        moving = parts[0]
        for step in range(1, NZ):
            total = send_ring(moving).astype(f32) + parts[step].astype(f32)
            moving = total.astype(bf16)
        rows = total.shape[0] // 2
        tile = (total[:rows] + send_mirror(moving[rows:]).astype(f32)).astype(bf16)
        tiles = [tile]
        for _ in range(1, NZ):
            tiles.append(send_ring(tiles[-1]))
        gathered = jnp.concatenate(tiles, 0)
        picked = jnp.dot(choice, gathered, preferred_element_type=f32).astype(bf16)
        for i, (dy, dc) in enumerate(OFFSETS):
            owned.append(send_group(picked[i * slots:(i + 1) * slots], dy, dc))
    outs = adamw(block_count, owned, master[0], moment1[0], moment2[0])
    return tuple(out[None] for out in outs)


def solution(mesh):
    fine = Mesh(mesh.devices.reshape(2, 4, NY, NZ, NC), ("zh", "x", "y", "z", "c"))
    pipe, edp = ("zh", "x"), ("y", "z", "c")
    shard = P(pipe, edp, None)
    tokens = P(pipe + edp, None)
    return jax.shard_map(
        per_device,
        mesh=fine,
        in_specs=(tokens, tokens, P(), P(), shard, shard, shard),
        out_specs=(shard, shard, shard),
        check_vma=False,
    )
```

```python
import functools
import jax
import jax.numpy as jnp
from jax import lax
from jax.experimental import pallas as pl
from jax.experimental.pallas import tpu as pltpu
from jax.sharding import Mesh, PartitionSpec as P

BLK = 8
CHUNKS = (512, 384)
NY, NZ, NC = 4, 4, 2
OFFSETS = tuple((dy, dc) for dy in range(NY) for dc in range(NC))

beta_first = 0.9
beta_second = 0.95
learn_rate = 0.00022
weight_decay = 0.1
adam_eps = 1e-08
bias_first = 1.0 - 0.9**20
bias_second = 1.0 - 0.95**20

bf16 = jnp.bfloat16
f32 = jnp.float32
VMEM = pl.BlockSpec(memory_space=pltpu.VMEM)
SMEM = pl.BlockSpec(memory_space=pltpu.SMEM)
ANY = pl.BlockSpec(memory_space=pl.ANY)
PARAMS = pltpu.CompilerParams(vmem_limit_bytes=40 * 1024 * 1024)


def send_group(value, dy, dc):
    if dy == 0 and dc == 0:
        return value
    pairs = []
    for y in range(NY):
        for c in range(NC):
            pairs.append((y * NC + c, (y + dy) % NY * NC + (c ^ dc)))
    return lax.ppermute(value, ("y", "c"), pairs)


def send_ring(value, steps):
    pairs = []
    for z in range(NZ):
        pairs.append((z, (z + steps) % NZ))
        pairs.append((NZ + z, NZ + (z + NZ - steps) % NZ))
    return lax.ppermute(value, ("zh", "z"), pairs)


def send_mirror(value):
    pairs = []
    for zh in range(2):
        for x in range(4):
            for z in range(NZ):
                source = (zh * 4 + x) * NZ + z
                target = ((1 - zh) * 4 + 3 - x) * NZ + NZ - 1 - z
                pairs.append((source, target))
    return lax.ppermute(value, ("zh", "x", "z"), pairs)


def ring_rank():
    z = lax.axis_index("z")
    return jnp.where(lax.axis_index("zh") == 0, z, NZ - 1 - z)


def prepare_kernel(live_ref, hidden_ref, out_ref):
    zh, x = lax.axis_index("zh"), lax.axis_index("x")
    y, z, c = lax.axis_index("y"), lax.axis_index("z"), lax.axis_index("c")
    live = live_ref[zh * 4 + x, (y * NZ + z) * NC + c]
    rank = jnp.where(zh == 0, z, NZ - 1 - z)
    rows = hidden_ref.shape[0]
    keep = lax.broadcasted_iota(jnp.int32, (128, rows), 1) < live
    for step in range(NZ):
        part = lax.rem(rank + 2 * NZ - 1 - step, NZ)
        for other in range(2):
            half = zh if other == 0 else 1 - zh
            block = (half * NZ + part) * 128
            cols = hidden_ref[:, pl.ds(pl.multiple_of(block, 128), 128)]
            turned = jnp.where(keep, cols.astype(f32).T, 0.0).astype(bf16)
            at = (step * 2 + other) * 128
            out_ref[at:at + 128, :] = turned


def prepare(hidden, live_tokens):
    return pl.pallas_call(
        prepare_kernel,
        out_shape=jax.ShapeDtypeStruct((hidden.shape[1], hidden.shape[0]), bf16),
        in_specs=[SMEM, VMEM],
        out_specs=VMEM,
        compiler_params=PARAMS,
        name="prepare",
    )(live_tokens, hidden)


def columns_of(y, c, base, cols):
    return pl.ds(pl.multiple_of((y * NC + c) * sum(CHUNKS) + base, 128), cols)


def pack_kernel(base, cols, grad_ref, after_ref, *rest):
    out_refs, sem = rest[:-1], rest[-1]
    y, c = lax.axis_index("y"), lax.axis_index("c")
    copies = []
    for i, out_ref in enumerate(out_refs):
        for other in range(NC):
            source = columns_of(lax.rem(y + i + 1, NY), lax.rem(c + other, NC), base, cols)
            copies.append(
                pltpu.make_async_copy(
                    grad_ref.at[:, source],
                    out_ref.at[:, other * cols:(other + 1) * cols],
                    sem.at[i * NC + other],
                )
            )
    for copy in copies:
        copy.start()
    for copy in copies:
        copy.wait()


def pack(grad, base, cols, after):
    shapes = [jax.ShapeDtypeStruct((grad.shape[0], NC * cols), bf16)] * (NY - 1)
    return pl.pallas_call(
        functools.partial(pack_kernel, base, cols),
        out_shape=shapes,
        in_specs=[ANY, ANY],
        out_specs=[ANY] * len(shapes),
        scratch_shapes=[pltpu.SemaphoreType.DMA((NC * len(shapes),))],
        compiler_params=PARAMS,
        name="pack",
    )(grad, after)


def product_kernel(base, cols, *refs):
    hidden, grad_ref, grads = refs[:NY], refs[NY], refs[NY + 1:2 * NY]
    outs, other_ref = refs[2 * NY:2 * NY + NZ], refs[2 * NY + NZ]
    left, right, sem = refs[2 * NY + NZ + 1:]
    y, c = lax.axis_index("y"), lax.axis_index("c")
    rows, depth = outs[0].shape[0], grad_ref.shape[0]
    copies = []
    for i in range(NY):
        tokens = slice(i * depth, (i + 1) * depth)
        copies.append((hidden[i], left.at[:, tokens]))
        if i:
            copies.append((grads[i - 1], right.at[tokens, :]))
        else:
            for other in range(NC):
                source = columns_of(y, lax.rem(c + other, NC), base, cols)
                target = right.at[tokens, other * cols:(other + 1) * cols]
                copies.append((grad_ref.at[:, source], target))
    copies = [pltpu.make_async_copy(a, b, sem.at[i]) for i, (a, b) in enumerate(copies)]
    for copy in copies:
        copy.start()
    for copy in copies:
        copy.wait()
    for step, out_ref in enumerate(outs):
        at = slice(step * rows, (step + 1) * rows)
        total = jnp.dot(left[at, :], right[...], preferred_element_type=f32)
        out_ref[...] = total[:, :cols].astype(bf16)
        other_ref[at, :] = total[:, cols:].astype(bf16)


def product(hidden, grad, grads, base, cols):
    width, tokens = hidden[0].shape
    depth = NY * tokens
    shapes = [jax.ShapeDtypeStruct((width // NZ, cols), bf16)] * NZ
    shapes.append(jax.ShapeDtypeStruct((width, cols), bf16))
    return pl.pallas_call(
        functools.partial(product_kernel, base, cols),
        out_shape=shapes,
        in_specs=[ANY] * (2 * NY),
        out_specs=[VMEM] * len(shapes),
        scratch_shapes=[
            pltpu.VMEM((width, depth), bf16),
            pltpu.VMEM((depth, NC * cols), bf16),
            pltpu.SemaphoreType.DMA((2 * NY + 1,)),
        ],
        compiler_params=PARAMS,
        cost_estimate=pl.CostEstimate(
            flops=2 * width * NC * cols * depth,
            bytes_accessed=2 * (width * (depth + NC * cols) + depth * NC * cols),
            transcendentals=0,
        ),
        name="product",
    )(*hidden, grad, *grads)


def adamw_kernel(*refs):
    counts_ref, owned_refs = refs[0], refs[1:1 + NY]
    master_ref, first_ref, second_ref, new_master_ref, new_first_ref, new_second_ref = refs[1 + NY:]
    zh, x = lax.axis_index("zh"), lax.axis_index("x")
    y, z, c = lax.axis_index("y"), lax.axis_index("z"), lax.axis_index("c")
    held = counts_ref[zh * 4 + x, (y * NZ + z) * NC + c]
    slots, cols = master_ref.shape[0], sum(CHUNKS)
    valid = lax.broadcasted_iota(jnp.int32, (slots, cols), 0) < held * BLK
    for dy in range(NY):
        for other in range(NC):
            at = columns_of(lax.rem(y + NY - dy, NY), lax.rem(c + other, NC), 0, cols)
            owned = owned_refs[dy][other].astype(f32)
            param = master_ref[:, at]
            first = beta_first * first_ref[:, at].astype(f32) + (1.0 - beta_first) * owned
            second = beta_second * second_ref[:, at].astype(f32) + (1.0 - beta_second) * owned * owned
            direction = first / bias_first / (jnp.sqrt(second / bias_second) + adam_eps)
            updated = param - learn_rate * (direction + weight_decay * param)
            new_master_ref[:, at] = jnp.where(valid, updated, 0.0)
            new_first_ref[:, at] = jnp.where(valid, first, 0.0).astype(bf16)
            new_second_ref[:, at] = jnp.where(valid, second, 0.0).astype(bf16)


def adamw(block_count, owned, master, moment1, moment2):
    shapes = [jax.ShapeDtypeStruct(a.shape, a.dtype) for a in (master, moment1, moment2)]
    return pl.pallas_call(
        adamw_kernel,
        out_shape=shapes,
        in_specs=[SMEM] + [VMEM] * (len(owned) + 3),
        out_specs=[VMEM] * 3,
        compiler_params=PARAMS,
        name="adamw",
    )(block_count, *owned, master, moment1, moment2)


def slot_choice(block_count, hblk, cap):
    y, z, c = lax.axis_index("y"), lax.axis_index("z"), lax.axis_index("c")
    counts = block_count[lax.axis_index("zh") * 4 + lax.axis_index("x")]
    owners = []
    for dy, dc in OFFSETS:
        owners.append(((y + dy) % NY * NZ + z) * NC + (c ^ dc))
    owners = jnp.stack(owners)
    before = jnp.arange(counts.shape[0], dtype=jnp.int32)[None, :] < owners[:, None]
    starts = jnp.sum(jnp.where(before, counts[None, :], 0), axis=1)
    slot = jnp.arange(cap, dtype=jnp.int32)
    block = jnp.minimum(starts[:, None] + slot[None, :], hblk - 1)
    per = hblk // NZ
    place = (ring_rank() + NZ - block // per) % NZ * per + block % per
    rows = place[:, :, None] * BLK + jnp.arange(BLK, dtype=jnp.int32)
    rows = rows.reshape(-1)
    return (rows[:, None] == jnp.arange(hblk * BLK, dtype=jnp.int32)[None, :]).astype(bf16)


def per_device(hidden_act, grad_out, live_tokens, block_count, master, moment1, moment2):
    half = hidden_act.shape[1] // 2
    slots = master.shape[1]
    turned = prepare(hidden_act, live_tokens)
    hidden = [send_group(turned, dy, 0) for dy in range(NY)]
    choice = slot_choice(block_count, half // BLK, slots // BLK)
    mine, swapped = [], []
    base = 0
    for k, cols in enumerate(CHUNKS):
        packed = pack(grad_out, base, cols, turned if k == 0 else hidden[1])
        grads = [send_group(packed[dy - 1], dy, 0) for dy in range(1, NY)]
        parts = product(hidden, grad_out, grads, base, cols)
        base += cols
        rows = parts[0].shape[0]
        sibling = send_group(parts[NZ], 0, 1)
        moving = None
        for step in range(NZ):
            total = parts[step].astype(f32) + sibling[step * rows:(step + 1) * rows].astype(f32)
            if step:
                total = total + send_ring(moving, 1).astype(f32)
            moving = total.astype(bf16)
        rows = rows // 2
        tile = (total[:rows] + send_mirror(moving[rows:]).astype(f32)).astype(bf16)
        gathered = jnp.concatenate([tile] + [send_ring(tile, d) for d in range(1, NZ)], 0)
        picked = jnp.dot(choice, gathered, preferred_element_type=f32).astype(bf16)
        picked = picked.reshape(NY, NC, slots, cols)
        mine.append(picked[:, 0])
        swapped.append(send_group(picked[:, 1], 0, 1))
    mine, swapped = jnp.concatenate(mine, 2), jnp.concatenate(swapped, 2)
    both = jnp.stack([mine, swapped], 1)
    owned = [send_group(both[dy], dy, 0) for dy in range(NY)]
    outs = adamw(block_count, owned, master[0], moment1[0], moment2[0])
    return tuple(out[None] for out in outs)


def solution(mesh):
    fine = Mesh(mesh.devices.reshape(2, 4, NY, NZ, NC), ("zh", "x", "y", "z", "c"))
    pipe, edp = ("zh", "x"), ("y", "z", "c")
    shard = P(pipe, edp, None)
    tokens = P(pipe + edp, None)
    return jax.shard_map(
        per_device,
        mesh=fine,
        in_specs=(tokens, tokens, P(), P(), shard, shard, shard),
        out_specs=(shard, shard, shard),
        check_vma=False,
    )
```

```python
import functools
import jax
import jax.numpy as jnp
from jax import lax
from jax.experimental import pallas as pl
from jax.experimental.pallas import tpu as pltpu
from jax.sharding import Mesh, PartitionSpec as P

BLK = 8
NY, NZ, NC = 4, 4, 2
NEAR = (1, NY - 1)
COLS, LATE = 896, 256
EARLY = COLS - LATE
LAG, FORWARD = 1, 1
OFFSETS = tuple((dy, dc) for dy in range(NY) for dc in range(NC))

beta_first = 0.9
beta_second = 0.95
learn_rate = 0.00022
weight_decay = 0.1
adam_eps = 1e-08
bias_first = 1.0 - 0.9**20
bias_second = 1.0 - 0.95**20

bf16 = jnp.bfloat16
f32 = jnp.float32
VMEM = pl.BlockSpec(memory_space=pltpu.VMEM)
SMEM = pl.BlockSpec(memory_space=pltpu.SMEM)
ANY = pl.BlockSpec(memory_space=pl.ANY)
HBM = pl.BlockSpec(memory_space=pltpu.HBM)
PARAMS = pltpu.CompilerParams(vmem_limit_bytes=40 * 1024 * 1024)
SMALL = pltpu.CompilerParams(vmem_limit_bytes=8 * 1024 * 1024)
FULL = pltpu.CompilerParams(vmem_limit_bytes=62 * 1024 * 1024)


def send_group(value, dy, dc):
    if dy == 0 and dc == 0:
        return value
    pairs = []
    for y in range(NY):
        for c in range(NC):
            pairs.append((y * NC + c, (y + dy) % NY * NC + (c ^ dc)))
    return lax.ppermute(value, ("y", "c"), pairs)


def send_ring(value, steps):
    pairs = []
    for z in range(NZ):
        pairs.append((z, (z + steps) % NZ))
        pairs.append((NZ + z, NZ + (z + NZ - steps) % NZ))
    return lax.ppermute(value, ("zh", "z"), pairs)


def send_mirror(value):
    pairs = []
    for zh in range(2):
        for x in range(4):
            for z in range(NZ):
                source = (zh * 4 + x) * NZ + z
                target = ((1 - zh) * 4 + 3 - x) * NZ + NZ - 1 - z
                pairs.append((source, target))
    return lax.ppermute(value, ("zh", "x", "z"), pairs)


def columns_of(y, c, base=0, cols=COLS):
    return pl.ds(pl.multiple_of((y * NC + c) * COLS + base, 128), cols)


def run(copies):
    for copy in copies:
        copy.start()
    for copy in copies:
        copy.wait()


def prepare_kernel(live_hbm, hidden_hbm, grad_hbm, own_hbm, up_hbm, down_hbm, swap_hbm, late_hbm, *rest):
    live_ref, hidden_ref, turned_ref, near_ref, late_ref, in_sem, out_sem = rest
    zh, x = lax.axis_index("zh"), lax.axis_index("x")
    y, z, c = lax.axis_index("y"), lax.axis_index("z"), lax.axis_index("c")
    rows, width = hidden_ref.shape
    pairs = [(hidden_hbm, hidden_ref), (live_hbm, live_ref)]
    for i, dy in enumerate(NEAR):
        for other in range(NC):
            source = columns_of(lax.rem(y + dy, NY), lax.rem(c + other, NC), 0, EARLY)
            pairs.append((grad_hbm.at[:, source], near_ref.at[i, :, other * EARLY:(other + 1) * EARLY]))
    for other in range(NC):
        for there in range(NY):
            source = columns_of(there, lax.rem(c + other, NC), EARLY, LATE)
            pairs.append((grad_hbm.at[:, source], late_ref.at[other, :, there * LATE:(there + 1) * LATE]))
    loads = [pltpu.make_async_copy(a, b, in_sem.at[i]) for i, (a, b) in enumerate(pairs)]
    for copy in loads:
        copy.start()
    loads[0].wait()
    loads[1].wait()
    live = live_ref[zh * 4 + x, (y * NZ + z) * NC + c]
    rank = jnp.where(zh == 0, z, NZ - 1 - z)
    keep = lax.broadcasted_iota(jnp.int32, (128, rows), 1) < live
    for own in range(2):
        half = zh if own else 1 - zh
        for step in range(NZ):
            part = lax.rem(rank + 2 * NZ - 1 - step, NZ)
            block = (half * NZ + part) * 128
            cols = hidden_ref[:, pl.ds(pl.multiple_of(block, 128), 128)]
            turned = jnp.where(keep, cols.astype(f32).T, 0.0).astype(bf16)
            at = own * NZ + step
            down, across = slice(at % 2 * 128, (at % 2 + 1) * 128), at // 2 * rows
            turned_ref[down, across:across + rows] = turned
    for copy in loads[2:]:
        copy.wait()
    pairs = [(turned_ref, own_hbm), (late_ref.at[0], late_hbm)]
    for out, grad in ((swap_hbm, late_ref.at[1]), (up_hbm, near_ref.at[0]), (down_hbm, near_ref.at[1])):
        pairs += [(turned_ref, out.at[:, :width]), (grad, out.at[:, width:])]
    run([pltpu.make_async_copy(a, b, out_sem.at[i]) for i, (a, b) in enumerate(pairs)])


def prepare(live_tokens, hidden, grad):
    rows, width = hidden.shape
    early, late = NC * EARLY, NY * LATE
    widths = [width, width + early, width + early, width + late, late]
    return pl.pallas_call(
        prepare_kernel,
        out_shape=[jax.ShapeDtypeStruct((rows, cols), bf16) for cols in widths],
        in_specs=[HBM] * 3,
        out_specs=[HBM] * 5,
        scratch_shapes=[
            pltpu.SMEM(live_tokens.shape, live_tokens.dtype),
            pltpu.VMEM(hidden.shape, bf16),
            pltpu.VMEM(hidden.shape, bf16),
            pltpu.VMEM((2, rows, early), bf16),
            pltpu.VMEM((NC, rows, late), bf16),
            pltpu.SemaphoreType.DMA((2 + 2 * NC + NC * NY,)),
            pltpu.SemaphoreType.DMA((8,)),
        ],
        compiler_params=FULL,
        name="prepare",
    )(live_tokens, hidden, grad)


def pack_kernel(grad_hbm, after_ref, far_hbm, own_hbm, buffer, in_sem, out_sem):
    y, c = lax.axis_index("y"), lax.axis_index("c")
    pairs = []
    for i, dy in enumerate((2, 0)):
        for other in range(NC):
            source = columns_of(lax.rem(y + dy, NY), lax.rem(c + other, NC), 0, EARLY)
            pairs.append((grad_hbm.at[:, source], buffer.at[i, :, other * EARLY:(other + 1) * EARLY]))
    run([pltpu.make_async_copy(a, b, in_sem.at[i]) for i, (a, b) in enumerate(pairs)])
    pairs = [(buffer.at[0], far_hbm), (buffer.at[1], own_hbm)]
    run([pltpu.make_async_copy(a, b, out_sem.at[i]) for i, (a, b) in enumerate(pairs)])


def pack(grad, after):
    shape = (grad.shape[0], NC * EARLY)
    return pl.pallas_call(
        pack_kernel,
        out_shape=[jax.ShapeDtypeStruct(shape, bf16)] * 2,
        in_specs=[HBM] * 2,
        out_specs=[HBM] * 2,
        scratch_shapes=[
            pltpu.VMEM((2,) + shape, bf16),
            pltpu.SemaphoreType.DMA((2 * NC,)),
            pltpu.SemaphoreType.DMA((2,)),
        ],
        compiler_params=FULL,
        name="pack",
    )(grad, after)


def forward_kernel(up_ref, down_ref, after_ref, far_up_ref, far_down_ref, sem):
    half = far_up_ref.shape[1]
    pairs = [(up_ref.at[:, :half], far_up_ref), (down_ref.at[:, half:2 * half], far_down_ref)]
    run([pltpu.make_async_copy(a, b, sem.at[i]) for i, (a, b) in enumerate(pairs)])


def forward(up, down, half, after):
    return pl.pallas_call(
        forward_kernel,
        out_shape=[jax.ShapeDtypeStruct((up.shape[0], half), bf16)] * 2,
        in_specs=[ANY] * 3,
        out_specs=[VMEM] * 2,
        scratch_shapes=[pltpu.SemaphoreType.DMA((2,))],
        compiler_params=SMALL,
        name="forward",
    )(up, down, after)


def chip_product_kernel(own_ref, late_ref, swap_ref, *rest):
    outs, (left, right, sem) = rest[:NZ], rest[NZ:]
    rows, width = own_ref.shape
    pairs = [
        (own_ref, left.at[0]),
        (swap_ref.at[:, :width], left.at[1]),
        (late_ref, right.at[:rows, :]),
        (swap_ref.at[:, width:], right.at[rows:, :]),
    ]
    run([pltpu.make_async_copy(a, b, sem.at[i]) for i, (a, b) in enumerate(pairs)])
    for block in range(NZ):
        at = slice(block * rows, (block + 1) * rows)
        both = jnp.concatenate([left[0, :, at], left[1, :, at]], 1)
        total = jnp.dot(both, right[...], preferred_element_type=f32).astype(bf16)
        half, step = block // 2, block % 2 * 2
        for i in range(2):
            outs[step + i][half * 128:(half + 1) * 128, :] = total[i * 128:(i + 1) * 128]


def chip_product(own, late, swap):
    rows, width = own.shape
    cols = late.shape[1]
    return pl.pallas_call(
        chip_product_kernel,
        out_shape=[jax.ShapeDtypeStruct((256, cols), bf16)] * NZ,
        in_specs=[ANY] * 3,
        out_specs=[VMEM] * NZ,
        scratch_shapes=[
            pltpu.VMEM((NC, rows, width), bf16),
            pltpu.VMEM((NC * rows, cols), bf16),
            pltpu.SemaphoreType.DMA((4,)),
        ],
        compiler_params=PARAMS,
        name="chip_product",
    )(own, late, swap)


def split_kernel(part_ref, moved_ref, *outs):
    y = lax.axis_index("y")
    for dy, out_ref in enumerate(outs):
        at = pl.ds(pl.multiple_of(lax.rem(y + dy, NY) * LATE, 128), LATE)
        total = part_ref[:, at].astype(f32) + moved_ref[:, at].astype(f32)
        out_ref[...] = total.astype(bf16)


def split(part, moved):
    return pl.pallas_call(
        split_kernel,
        out_shape=[jax.ShapeDtypeStruct((part.shape[0], LATE), bf16)] * NY,
        in_specs=[VMEM] * 2,
        out_specs=[VMEM] * NY,
        compiler_params=SMALL,
        name="split",
    )(part, moved)


def product_kernel(part, n_after, *refs):
    hidden, grads = refs[:NY + 1], refs[NY + 1:2 * NY + 1]
    refs = refs[2 * NY + 1 + n_after:]
    outs, other_ref, (left, right, sem) = refs[:NZ], refs[NZ], refs[NZ + 1:]
    depth, width = hidden[0].shape
    rows, lead = outs[0].shape[0], part * width // 2
    pairs = []
    for dy in range(NY):
        if dy == 2:
            piece = hidden[NY] if part else hidden[2]
        else:
            piece = hidden[dy].at[:, lead:lead + width // 2]
        pairs.append((piece, left.at[dy]))
        first = grads[dy].shape[1] - NC * EARLY
        pairs.append((grads[dy].at[:, first:], right.at[dy * depth:(dy + 1) * depth, :]))
    run([pltpu.make_async_copy(a, b, sem.at[i]) for i, (a, b) in enumerate(pairs)])
    for pair in range(NZ // 2):
        at = slice(pair * depth, (pair + 1) * depth)
        block = jnp.concatenate([left[i, :, at] for i in range(NY)], 1)
        total = jnp.dot(block, right[...], preferred_element_type=f32)
        for i in range(2):
            outs[pair * 2 + i][...] = total[i * rows:(i + 1) * rows, :EARLY].astype(bf16)
        other_ref[pair * 2 * rows:(pair + 1) * 2 * rows, :] = total[:, EARLY:].astype(bf16)


def product(part, hidden, grads, after):
    tokens, width = hidden[0].shape
    depth, rows = NY * tokens, width // 2 // NZ
    shapes = [jax.ShapeDtypeStruct((rows, EARLY), bf16)] * NZ
    shapes.append(jax.ShapeDtypeStruct((rows * NZ, EARLY), bf16))
    return pl.pallas_call(
        functools.partial(product_kernel, part, len(after)),
        out_shape=shapes,
        in_specs=[ANY] * (2 * NY + 1 + len(after)),
        out_specs=[VMEM] * len(shapes),
        scratch_shapes=[
            pltpu.VMEM((NY, tokens, width // 2), bf16),
            pltpu.VMEM((depth, NC * EARLY), bf16),
            pltpu.SemaphoreType.DMA((2 * NY,)),
        ],
        compiler_params=PARAMS,
        cost_estimate=pl.CostEstimate(
            flops=width * NC * EARLY * depth,
            bytes_accessed=width * (depth + NC * EARLY) + 2 * depth * NC * EARLY,
            transcendentals=0,
        ),
        name="product",
    )(*hidden, *grads, *after)


def add_kernel(terms, pieces, *refs):
    out_ref, rows = refs[-1], refs[-1].shape[0]
    total = None
    for ref, at in zip(refs, terms):
        term = ref[at:at + rows, :].astype(f32)
        total = term if total is None else total + term
    out_ref[:, :total.shape[1]] = total.astype(out_ref.dtype)
    if pieces is not None:
        total = None
        for ref in refs[len(terms):len(terms) + NY]:
            term = ref[pieces:pieces + rows, :].astype(f32)
            total = term if total is None else total + term
        out_ref[:, out_ref.shape[1] - total.shape[1]:] = total.astype(out_ref.dtype)


def add(terms, dtype, after=(), late=(), at=None, rows=128):
    cols = terms[0][0].shape[1] + (late[0].shape[1] if late else 0)
    return pl.pallas_call(
        functools.partial(add_kernel, tuple(first for _, first in terms), at),
        out_shape=jax.ShapeDtypeStruct((rows, cols), dtype),
        in_specs=[VMEM] * (len(terms) + len(late)) + [ANY] * len(after),
        out_specs=VMEM,
        compiler_params=SMALL,
        name="add",
    )(*[value for value, _ in terms], *late, *after)


def adamw_kernel(*refs):
    counts_ref, owned_refs = refs[0], refs[1:1 + NY]
    master_ref, first_ref, second_ref, new_master_ref, new_first_ref, new_second_ref = refs[1 + NY:]
    zh, x = lax.axis_index("zh"), lax.axis_index("x")
    y, z, c = lax.axis_index("y"), lax.axis_index("z"), lax.axis_index("c")
    held = counts_ref[zh * 4 + x, (y * NZ + z) * NC + c]
    slots, cols = master_ref.shape[0], COLS
    valid = lax.broadcasted_iota(jnp.int32, (slots, cols), 0) < held * BLK
    for dy in range(NY):
        for other in range(NC):
            at = columns_of(lax.rem(y + NY - dy, NY), lax.rem(c + other, NC))
            owned = owned_refs[dy][other].astype(f32)
            param = master_ref[:, at]
            first = beta_first * first_ref[:, at].astype(f32) + (1.0 - beta_first) * owned
            second = beta_second * second_ref[:, at].astype(f32) + (1.0 - beta_second) * owned * owned
            direction = first / bias_first / (jnp.sqrt(second / bias_second) + adam_eps)
            updated = param - learn_rate * (direction + weight_decay * param)
            new_master_ref[:, at] = jnp.where(valid, updated, 0.0)
            new_first_ref[:, at] = jnp.where(valid, first, 0.0).astype(bf16)
            new_second_ref[:, at] = jnp.where(valid, second, 0.0).astype(bf16)


def adamw(block_count, owned, master, moment1, moment2):
    shapes = [jax.ShapeDtypeStruct(a.shape, a.dtype) for a in (master, moment1, moment2)]
    return pl.pallas_call(
        adamw_kernel,
        out_shape=shapes,
        in_specs=[SMEM] + [VMEM] * (len(owned) + 3),
        out_specs=[VMEM] * 3,
        compiler_params=PARAMS,
        name="adamw",
    )(block_count, *owned, master, moment1, moment2)


def slot_choice(block_count, hblk, cap):
    y, z, c = lax.axis_index("y"), lax.axis_index("z"), lax.axis_index("c")
    counts = block_count[lax.axis_index("zh") * 4 + lax.axis_index("x")]
    owners = []
    for dy, dc in OFFSETS:
        owners.append(((y + dy) % NY * NZ + z) * NC + (c ^ dc))
    owners = jnp.stack(owners)
    before = jnp.arange(counts.shape[0], dtype=jnp.int32)[None, :] < owners[:, None]
    starts = jnp.sum(jnp.where(before, counts[None, :], 0), axis=1)
    slot = jnp.arange(cap, dtype=jnp.int32)
    block = jnp.minimum(starts[:, None] + slot[None, :], hblk - 1)
    per = hblk // NZ
    chunk = block // per
    chunk = jnp.where(lax.axis_index("zh") == 0, chunk, NZ - 1 - chunk)
    place = chunk * per + block % per
    rows = place[:, :, None] * BLK + jnp.arange(BLK, dtype=jnp.int32)
    rows = rows.reshape(-1)
    return (rows[:, None] == jnp.arange(hblk * BLK, dtype=jnp.int32)[None, :]).astype(bf16)


def per_device(hidden_act, grad_out, live_tokens, block_count, master, moment1, moment2):
    half = hidden_act.shape[1] // 2
    slots = master.shape[1]
    own, up, down, swap, late = prepare(live_tokens, hidden_act, grad_out)
    choice = slot_choice(block_count, half // BLK, slots // BLK)
    near = [send_group(up, 1, 0), send_group(down, 3, 0)]
    opposite, mine = pack(grad_out, own)
    grads = [mine, near[0], send_group(opposite, 2, 0), near[1]]

    parts = chip_product(own, late, send_group(swap, 0, 1))
    moving, steps = parts[0], []
    for step in range(1, NZ - 1):
        moving = add([(parts[step], 0), (send_ring(moving, 1), 0)], bf16, rows=256)
        steps.append(moving)
    pieces = split(parts[NZ - 1], send_ring(moving, 1))
    late = [send_group(piece, dy, 0) for dy, piece in enumerate(pieces)]

    far = forward(near[0], near[1], half, steps[FORWARD])
    far = [send_group(far[0], 1, 0), send_group(far[1], 3, 0)]
    hidden = [own, near[0], far[0], near[1], far[1]]
    sums, after = [], [pieces[0]]
    for part in range(2):
        parts = product(part, hidden, grads, [] if part else after)
        sibling = send_group(parts[NZ], 0, 1)
        moved = []
        for step in range(NZ):
            terms = [(parts[step], 0), (sibling, step * 128)] + moved
            if step < NZ - 1:
                total = add(terms, bf16, after if part and not step else ())
                moved = [(send_ring(total, 1), 0)]
            else:
                total = add(terms, f32 if part else bf16, (), late, part * 128)
            if step == LAG:
                after = [total]
        sums.append(total)
    tile = (sums[1] + send_mirror(sums[0]).astype(f32)).astype(bf16)
    gathered = lax.all_gather(tile, "z", axis=0, tiled=True)
    picked = jnp.dot(choice, gathered, preferred_element_type=f32).astype(bf16)
    picked = picked.reshape(NY, NC, slots, COLS)
    both = jnp.stack([picked[:, 0], send_group(picked[:, 1], 0, 1)], 1)
    owned = [send_group(both[dy], dy, 0) for dy in range(NY)]
    outs = adamw(block_count, owned, master[0], moment1[0], moment2[0])
    return tuple(out[None] for out in outs)


def solution(mesh):
    fine = Mesh(mesh.devices.reshape(2, 4, NY, NZ, NC), ("zh", "x", "y", "z", "c"))
    pipe, edp = ("zh", "x"), ("y", "z", "c")
    shard = P(pipe, edp, None)
    tokens = P(pipe + edp, None)
    return jax.shard_map(
        per_device,
        mesh=fine,
        in_specs=(tokens, tokens, P(), P(), shard, shard, shard),
        out_specs=(shard, shard, shard),
        check_vma=False,
    )
```

```python
import functools
import jax
import jax.numpy as jnp
from jax import lax
from jax.experimental import pallas as pl
from jax.experimental.pallas import tpu as pltpu
from jax.sharding import Mesh, PartitionSpec as P

BLK = 8
NY, NZ, NC = 4, 4, 2
NEAR = (1, NY - 1)
COLS, LATE = 896, 256
EARLY = COLS - LATE
LAG, FORWARD = 0, 1
COST = 1
OFFSETS = tuple((dy, dc) for dy in range(NY) for dc in range(NC))

beta_first = 0.9
beta_second = 0.95
learn_rate = 0.00022
weight_decay = 0.1
adam_eps = 1e-08
bias_first = 1.0 - 0.9**20
bias_second = 1.0 - 0.95**20

bf16 = jnp.bfloat16
f32 = jnp.float32
VMEM = pl.BlockSpec(memory_space=pltpu.VMEM)
SMEM = pl.BlockSpec(memory_space=pltpu.SMEM)
ANY = pl.BlockSpec(memory_space=pl.ANY)
HBM = pl.BlockSpec(memory_space=pltpu.HBM)
PARAMS = pltpu.CompilerParams(vmem_limit_bytes=40 * 1024 * 1024)
SMALL = pltpu.CompilerParams(vmem_limit_bytes=8 * 1024 * 1024)
FULL = pltpu.CompilerParams(vmem_limit_bytes=62 * 1024 * 1024)


def send_group(value, dy, dc):
    if dy == 0 and dc == 0:
        return value
    pairs = []
    for y in range(NY):
        for c in range(NC):
            pairs.append((y * NC + c, (y + dy) % NY * NC + (c ^ dc)))
    return lax.ppermute(value, ("y", "c"), pairs)


def send_ring(value, steps):
    pairs = []
    for z in range(NZ):
        pairs.append((z, (z + steps) % NZ))
        pairs.append((NZ + z, NZ + (z + NZ - steps) % NZ))
    return lax.ppermute(value, ("zh", "z"), pairs)


def send_mirror(value):
    pairs = []
    for zh in range(2):
        for x in range(4):
            for z in range(NZ):
                source = (zh * 4 + x) * NZ + z
                target = ((1 - zh) * 4 + 3 - x) * NZ + NZ - 1 - z
                pairs.append((source, target))
    return lax.ppermute(value, ("zh", "x", "z"), pairs)


def columns_of(y, c, base=0, cols=COLS):
    return pl.ds(pl.multiple_of((y * NC + c) * COLS + base, 128), cols)


def run(copies):
    for copy in copies:
        copy.start()
    for copy in copies:
        copy.wait()


def prepare_kernel(live_hbm, hidden_hbm, grad_hbm, own_hbm, up_hbm, down_hbm, swap_hbm, late_hbm, *rest):
    live_ref, hidden_ref, turned_ref, near_ref, late_ref, in_sem, out_sem = rest
    zh, x = lax.axis_index("zh"), lax.axis_index("x")
    y, z, c = lax.axis_index("y"), lax.axis_index("z"), lax.axis_index("c")
    rows, width = hidden_ref.shape
    pairs = [(hidden_hbm, hidden_ref), (live_hbm, live_ref)]
    for i, dy in enumerate(NEAR):
        for other in range(NC):
            source = columns_of(lax.rem(y + dy, NY), lax.rem(c + other, NC), 0, EARLY)
            pairs.append((grad_hbm.at[:, source], near_ref.at[i, :, other * EARLY:(other + 1) * EARLY]))
    for other in range(NC):
        for there in range(NY):
            source = columns_of(there, lax.rem(c + other, NC), EARLY, LATE)
            pairs.append((grad_hbm.at[:, source], late_ref.at[other, :, there * LATE:(there + 1) * LATE]))
    loads = [pltpu.make_async_copy(a, b, in_sem.at[i]) for i, (a, b) in enumerate(pairs)]
    for copy in loads:
        copy.start()
    loads[0].wait()
    loads[1].wait()
    live = live_ref[zh * 4 + x, (y * NZ + z) * NC + c]
    rank = jnp.where(zh == 0, z, NZ - 1 - z)
    keep = lax.broadcasted_iota(jnp.int32, (128, rows), 1) < live
    for own in range(2):
        half = zh if own else 1 - zh
        for step in range(NZ):
            part = lax.rem(rank + 2 * NZ - 1 - step, NZ)
            block = (half * NZ + part) * 128
            cols = hidden_ref[:, pl.ds(pl.multiple_of(block, 128), 128)]
            turned = jnp.where(keep, cols.astype(f32).T, 0.0).astype(bf16)
            at = own * NZ + step
            down, across = slice(at % 2 * 128, (at % 2 + 1) * 128), at // 2 * rows
            turned_ref[down, across:across + rows] = turned
    for copy in loads[2:]:
        copy.wait()
    pairs = [(turned_ref, own_hbm), (late_ref.at[0], late_hbm)]
    for out, grad in ((swap_hbm, late_ref.at[1]), (up_hbm, near_ref.at[0]), (down_hbm, near_ref.at[1])):
        pairs += [(turned_ref, out.at[:, :width]), (grad, out.at[:, width:])]
    run([pltpu.make_async_copy(a, b, out_sem.at[i]) for i, (a, b) in enumerate(pairs)])


def prepare(live_tokens, hidden, grad):
    rows, width = hidden.shape
    early, late = NC * EARLY, NY * LATE
    widths = [width, width + early, width + early, width + late, late]
    return pl.pallas_call(
        prepare_kernel,
        out_shape=[jax.ShapeDtypeStruct((rows, cols), bf16) for cols in widths],
        in_specs=[HBM] * 3,
        out_specs=[HBM] * 5,
        scratch_shapes=[
            pltpu.SMEM(live_tokens.shape, live_tokens.dtype),
            pltpu.VMEM(hidden.shape, bf16),
            pltpu.VMEM(hidden.shape, bf16),
            pltpu.VMEM((2, rows, early), bf16),
            pltpu.VMEM((NC, rows, late), bf16),
            pltpu.SemaphoreType.DMA((2 + 2 * NC + NC * NY,)),
            pltpu.SemaphoreType.DMA((8,)),
        ],
        compiler_params=FULL,
        name="prepare",
    )(live_tokens, hidden, grad)


def pack_kernel(grad_hbm, after_ref, far_hbm, own_hbm, buffer, in_sem, out_sem):
    y, c = lax.axis_index("y"), lax.axis_index("c")
    pairs = []
    for i, dy in enumerate((2, 0)):
        for other in range(NC):
            source = columns_of(lax.rem(y + dy, NY), lax.rem(c + other, NC), 0, EARLY)
            pairs.append((grad_hbm.at[:, source], buffer.at[i, :, other * EARLY:(other + 1) * EARLY]))
    run([pltpu.make_async_copy(a, b, in_sem.at[i]) for i, (a, b) in enumerate(pairs)])
    pairs = [(buffer.at[0], far_hbm), (buffer.at[1], own_hbm)]
    run([pltpu.make_async_copy(a, b, out_sem.at[i]) for i, (a, b) in enumerate(pairs)])


def pack(grad, after):
    shape = (grad.shape[0], NC * EARLY)
    return pl.pallas_call(
        pack_kernel,
        out_shape=[jax.ShapeDtypeStruct(shape, bf16)] * 2,
        in_specs=[HBM] * 2,
        out_specs=[HBM] * 2,
        scratch_shapes=[
            pltpu.VMEM((2,) + shape, bf16),
            pltpu.SemaphoreType.DMA((2 * NC,)),
            pltpu.SemaphoreType.DMA((2,)),
        ],
        compiler_params=FULL,
        name="pack",
    )(grad, after)


def forward_kernel(up_ref, down_ref, after_ref, far_up_ref, far_down_ref, sem):
    half = far_up_ref.shape[1]
    pairs = [(up_ref.at[:, :half], far_up_ref), (down_ref.at[:, half:2 * half], far_down_ref)]
    run([pltpu.make_async_copy(a, b, sem.at[i]) for i, (a, b) in enumerate(pairs)])


def forward(up, down, half, after):
    return pl.pallas_call(
        forward_kernel,
        out_shape=[jax.ShapeDtypeStruct((up.shape[0], half), bf16)] * 2,
        in_specs=[ANY] * 3,
        out_specs=[VMEM] * 2,
        scratch_shapes=[pltpu.SemaphoreType.DMA((2,))],
        compiler_params=SMALL,
        name="forward",
    )(up, down, after)


def chip_product_kernel(own_ref, late_ref, swap_ref, *rest):
    outs, (left, right, sem) = rest[:2 * NZ], rest[2 * NZ:]
    rows, width = own_ref.shape
    pairs = [
        (own_ref, left.at[0]),
        (swap_ref.at[:, :width], left.at[1]),
        (late_ref, right.at[:rows, :]),
        (swap_ref.at[:, width:], right.at[rows:, :]),
    ]
    run([pltpu.make_async_copy(a, b, sem.at[i]) for i, (a, b) in enumerate(pairs)])
    for block in range(NZ):
        at = slice(block * rows, (block + 1) * rows)
        both = jnp.concatenate([left[0, :, at], left[1, :, at]], 1)
        total = jnp.dot(both, right[...], preferred_element_type=f32).astype(bf16)
        for i in range(2):
            outs[block * 2 + i][...] = total[i * 128:(i + 1) * 128]


def chip_product(own, late, swap):
    rows, width = own.shape
    cols = late.shape[1]
    return pl.pallas_call(
        chip_product_kernel,
        out_shape=[jax.ShapeDtypeStruct((128, cols), bf16)] * (2 * NZ),
        in_specs=[ANY] * 3,
        out_specs=[VMEM] * (2 * NZ),
        scratch_shapes=[
            pltpu.VMEM((NC, rows, width), bf16),
            pltpu.VMEM((NC * rows, cols), bf16),
            pltpu.SemaphoreType.DMA((4,)),
        ],
        compiler_params=PARAMS,
        name="chip_product",
    )(own, late, swap)


def split_kernel(*refs):
    y = lax.axis_index("y")
    for half in range(2):
        part_ref, moved_ref = refs[2 * half], refs[2 * half + 1]
        for dy, out_ref in enumerate(refs[4:]):
            at = pl.ds(pl.multiple_of(lax.rem(y + dy, NY) * LATE, 128), LATE)
            total = part_ref[:, at].astype(f32) + moved_ref[:, at].astype(f32)
            out_ref[half * 128:(half + 1) * 128, :] = total.astype(bf16)


def split(*terms):
    return pl.pallas_call(
        split_kernel,
        out_shape=[jax.ShapeDtypeStruct((256, LATE), bf16)] * NY,
        in_specs=[VMEM] * 4,
        out_specs=[VMEM] * NY,
        compiler_params=SMALL,
        name="split",
    )(*terms)


def product_kernel(part, n_after, *refs):
    hidden, grads = refs[:NY + 1], refs[NY + 1:2 * NY + 1]
    refs = refs[2 * NY + 1 + n_after:]
    outs, other_ref, (left, right, sem) = refs[:NZ], refs[NZ], refs[NZ + 1:]
    depth, width = hidden[0].shape
    rows, lead = outs[0].shape[0], part * width // 2
    pairs = []
    for dy in range(NY):
        if dy == 2:
            piece = hidden[NY] if part else hidden[2]
        else:
            piece = hidden[dy].at[:, lead:lead + width // 2]
        pairs.append((piece, left.at[dy]))
        first = grads[dy].shape[1] - NC * EARLY
        pairs.append((grads[dy].at[:, first:], right.at[dy * depth:(dy + 1) * depth, :]))
    run([pltpu.make_async_copy(a, b, sem.at[i]) for i, (a, b) in enumerate(pairs)])
    for pair in range(NZ // 2):
        at = slice(pair * depth, (pair + 1) * depth)
        block = jnp.concatenate([left[i, :, at] for i in range(NY)], 1)
        total = jnp.dot(block, right[...], preferred_element_type=f32)
        for i in range(2):
            outs[pair * 2 + i][...] = total[i * rows:(i + 1) * rows, :EARLY].astype(bf16)
        other_ref[pair * 2 * rows:(pair + 1) * 2 * rows, :] = total[:, EARLY:].astype(bf16)


def product(part, hidden, grads, after):
    tokens, width = hidden[0].shape
    depth, rows = NY * tokens, width // 2 // NZ
    shapes = [jax.ShapeDtypeStruct((rows, EARLY), bf16)] * NZ
    shapes.append(jax.ShapeDtypeStruct((rows * NZ, EARLY), bf16))
    return pl.pallas_call(
        functools.partial(product_kernel, part, len(after)),
        out_shape=shapes,
        in_specs=[ANY] * (2 * NY + 1 + len(after)),
        out_specs=[VMEM] * len(shapes),
        scratch_shapes=[
            pltpu.VMEM((NY, tokens, width // 2), bf16),
            pltpu.VMEM((depth, NC * EARLY), bf16),
            pltpu.SemaphoreType.DMA((2 * NY,)),
        ],
        compiler_params=PARAMS,
        cost_estimate=pl.CostEstimate(
            flops=COST * width * NC * EARLY * depth,
            bytes_accessed=width * (depth + NC * EARLY) + 2 * depth * NC * EARLY,
            transcendentals=0,
        ),
        name="product",
    )(*hidden, *grads, *after)


def add_kernel(terms, pieces, *refs):
    out_ref, rows = refs[-1], refs[-1].shape[0]
    total = None
    for ref, at in zip(refs, terms):
        term = ref[at:at + rows, :].astype(f32)
        total = term if total is None else total + term
    out_ref[:, :total.shape[1]] = total.astype(out_ref.dtype)
    if pieces is not None:
        total = None
        for ref in refs[len(terms):len(terms) + NY]:
            term = ref[pieces:pieces + rows, :].astype(f32)
            total = term if total is None else total + term
        out_ref[:, out_ref.shape[1] - total.shape[1]:] = total.astype(out_ref.dtype)


def add(terms, dtype, after=(), late=(), at=None, rows=128):
    cols = terms[0][0].shape[1] + (late[0].shape[1] if late else 0)
    return pl.pallas_call(
        functools.partial(add_kernel, tuple(first for _, first in terms), at),
        out_shape=jax.ShapeDtypeStruct((rows, cols), dtype),
        in_specs=[VMEM] * (len(terms) + len(late)) + [ANY] * len(after),
        out_specs=VMEM,
        compiler_params=SMALL,
        name="add",
    )(*[value for value, _ in terms], *late, *after)


def adamw_kernel(*refs):
    counts_ref, owned_refs = refs[0], refs[1:1 + NY]
    master_ref, first_ref, second_ref, new_master_ref, new_first_ref, new_second_ref = refs[1 + NY:]
    zh, x = lax.axis_index("zh"), lax.axis_index("x")
    y, z, c = lax.axis_index("y"), lax.axis_index("z"), lax.axis_index("c")
    held = counts_ref[zh * 4 + x, (y * NZ + z) * NC + c]
    slots, cols = master_ref.shape[0], COLS
    valid = lax.broadcasted_iota(jnp.int32, (slots, cols), 0) < held * BLK
    for dy in range(NY):
        for other in range(NC):
            at = columns_of(lax.rem(y + NY - dy, NY), lax.rem(c + other, NC))
            owned = owned_refs[dy][other].astype(f32)
            param = master_ref[:, at]
            first = beta_first * first_ref[:, at].astype(f32) + (1.0 - beta_first) * owned
            second = beta_second * second_ref[:, at].astype(f32) + (1.0 - beta_second) * owned * owned
            direction = first / bias_first / (jnp.sqrt(second / bias_second) + adam_eps)
            updated = param - learn_rate * (direction + weight_decay * param)
            new_master_ref[:, at] = jnp.where(valid, updated, 0.0)
            new_first_ref[:, at] = jnp.where(valid, first, 0.0).astype(bf16)
            new_second_ref[:, at] = jnp.where(valid, second, 0.0).astype(bf16)


def adamw(block_count, owned, master, moment1, moment2):
    shapes = [jax.ShapeDtypeStruct(a.shape, a.dtype) for a in (master, moment1, moment2)]
    return pl.pallas_call(
        adamw_kernel,
        out_shape=shapes,
        in_specs=[SMEM] + [VMEM] * (len(owned) + 3),
        out_specs=[VMEM] * 3,
        compiler_params=PARAMS,
        name="adamw",
    )(block_count, *owned, master, moment1, moment2)


def slot_choice(block_count, hblk, cap):
    y, z, c = lax.axis_index("y"), lax.axis_index("z"), lax.axis_index("c")
    counts = block_count[lax.axis_index("zh") * 4 + lax.axis_index("x")]
    owners = []
    for dy, dc in OFFSETS:
        owners.append(((y + dy) % NY * NZ + z) * NC + (c ^ dc))
    owners = jnp.stack(owners)
    before = jnp.arange(counts.shape[0], dtype=jnp.int32)[None, :] < owners[:, None]
    starts = jnp.sum(jnp.where(before, counts[None, :], 0), axis=1)
    slot = jnp.arange(cap, dtype=jnp.int32)
    block = jnp.minimum(starts[:, None] + slot[None, :], hblk - 1)
    per = hblk // NZ
    chunk = block // per
    chunk = jnp.where(lax.axis_index("zh") == 0, chunk, NZ - 1 - chunk)
    place = chunk * per + block % per
    rows = place[:, :, None] * BLK + jnp.arange(BLK, dtype=jnp.int32)
    rows = rows.reshape(-1)
    return (rows[:, None] == jnp.arange(hblk * BLK, dtype=jnp.int32)[None, :]).astype(bf16)


def per_device(hidden_act, grad_out, live_tokens, block_count, master, moment1, moment2):
    half = hidden_act.shape[1] // 2
    slots = master.shape[1]
    own, up, down, swap, late = prepare(live_tokens, hidden_act, grad_out)
    choice = slot_choice(block_count, half // BLK, slots // BLK)
    near = [send_group(up, 1, 0), send_group(down, 3, 0)]
    opposite, mine = pack(grad_out, own)
    grads = [mine, near[0], send_group(opposite, 2, 0), near[1]]

    parts = chip_product(own, late, send_group(swap, 0, 1))
    moving, steps = [parts[0], parts[NZ]], []
    for step in range(1, NZ - 1):
        moving = [
            add([(parts[half * NZ + step], 0), (send_ring(moving[half], 1), 0)], bf16)
            for half in range(2)
        ]
        steps.append(moving[1])
    pieces = split(
        parts[NZ - 1], send_ring(moving[0], 1), parts[2 * NZ - 1], send_ring(moving[1], 1)
    )
    late = [send_group(piece, dy, 0) for dy, piece in enumerate(pieces)]

    far = forward(near[0], near[1], half, steps[FORWARD])
    far = [send_group(far[0], 1, 0), send_group(far[1], 3, 0)]
    hidden = [own, near[0], far[0], near[1], far[1]]
    sums, after = [], [pieces[0]]
    for part in range(2):
        parts = product(part, hidden, grads, [] if part else after)
        sibling = send_group(parts[NZ], 0, 1)
        moved = []
        for step in range(NZ):
            terms = [(parts[step], 0), (sibling, step * 128)] + moved
            if step < NZ - 1:
                total = add(terms, bf16, after if part and not step else ())
                moved = [(send_ring(total, 1), 0)]
            else:
                total = add(terms, f32 if part else bf16, (), late, part * 128)
            if step == LAG:
                after = [total]
        sums.append(total)
    tile = (sums[1] + send_mirror(sums[0]).astype(f32)).astype(bf16)
    gathered = lax.all_gather(tile, "z", axis=0, tiled=True)
    picked = jnp.dot(choice, gathered, preferred_element_type=f32).astype(bf16)
    picked = picked.reshape(NY, NC, slots, COLS)
    both = jnp.stack([picked[:, 0], send_group(picked[:, 1], 0, 1)], 1)
    owned = [send_group(both[dy], dy, 0) for dy in range(NY)]
    outs = adamw(block_count, owned, master[0], moment1[0], moment2[0])
    return tuple(out[None] for out in outs)


def solution(mesh):
    fine = Mesh(mesh.devices.reshape(2, 4, NY, NZ, NC), ("zh", "x", "y", "z", "c"))
    pipe, edp = ("zh", "x"), ("y", "z", "c")
    shard = P(pipe, edp, None)
    tokens = P(pipe + edp, None)
    return jax.shard_map(
        per_device,
        mesh=fine,
        in_specs=(tokens, tokens, P(), P(), shard, shard, shard),
        out_specs=(shard, shard, shard),
        check_vma=False,
    )
```

```python
import functools
import jax
import jax.numpy as jnp
from jax import lax
from jax.experimental import pallas as pl
from jax.experimental.pallas import tpu as pltpu
from jax.sharding import Mesh, PartitionSpec as P

BLK = 8
NY, NZ, NC = 4, 4, 2
NEAR = (1, NY - 1)
COLS, LATE = 896, 256
EARLY = COLS - LATE
LAG, FORWARD = 0, 1
COST = 1
OFFSETS = tuple((dy, dc) for dy in range(NY) for dc in range(NC))

beta_first = 0.9
beta_second = 0.95
learn_rate = 0.00022
weight_decay = 0.1
adam_eps = 1e-08
bias_first = 1.0 - 0.9**20
bias_second = 1.0 - 0.95**20

bf16 = jnp.bfloat16
f32 = jnp.float32
VMEM = pl.BlockSpec(memory_space=pltpu.VMEM)
SMEM = pl.BlockSpec(memory_space=pltpu.SMEM)
ANY = pl.BlockSpec(memory_space=pl.ANY)
HBM = pl.BlockSpec(memory_space=pltpu.HBM)
PARAMS = pltpu.CompilerParams(vmem_limit_bytes=40 * 1024 * 1024)
SMALL = pltpu.CompilerParams(vmem_limit_bytes=8 * 1024 * 1024)
FULL = pltpu.CompilerParams(vmem_limit_bytes=62 * 1024 * 1024)


def send_group(value, dy, dc):
    if dy == 0 and dc == 0:
        return value
    pairs = []
    for y in range(NY):
        for c in range(NC):
            pairs.append((y * NC + c, (y + dy) % NY * NC + (c ^ dc)))
    return lax.ppermute(value, ("y", "c"), pairs)


def send_ring(value, steps):
    pairs = []
    for z in range(NZ):
        pairs.append((z, (z + steps) % NZ))
        pairs.append((NZ + z, NZ + (z + NZ - steps) % NZ))
    return lax.ppermute(value, ("zh", "z"), pairs)


def send_mirror(value):
    pairs = []
    for zh in range(2):
        for x in range(4):
            for z in range(NZ):
                source = (zh * 4 + x) * NZ + z
                target = ((1 - zh) * 4 + 3 - x) * NZ + NZ - 1 - z
                pairs.append((source, target))
    return lax.ppermute(value, ("zh", "x", "z"), pairs)


def columns_of(y, c, base=0, cols=COLS):
    return pl.ds(pl.multiple_of((y * NC + c) * COLS + base, 128), cols)


def run(copies):
    for copy in copies:
        copy.start()
    for copy in copies:
        copy.wait()


def prepare_kernel(live_hbm, hidden_hbm, grad_hbm, own_hbm, up_hbm, down_hbm, swap_hbm, late_hbm, *rest):
    live_ref, hidden_ref, turned_ref, near_ref, late_ref, in_sem, out_sem = rest
    zh, x = lax.axis_index("zh"), lax.axis_index("x")
    y, z, c = lax.axis_index("y"), lax.axis_index("z"), lax.axis_index("c")
    rows, width = hidden_ref.shape
    pairs = [(hidden_hbm, hidden_ref), (live_hbm, live_ref)]
    for i, dy in enumerate(NEAR):
        for other in range(NC):
            source = columns_of(lax.rem(y + dy, NY), lax.rem(c + other, NC), 0, EARLY)
            pairs.append((grad_hbm.at[:, source], near_ref.at[i, :, other * EARLY:(other + 1) * EARLY]))
    for other in range(NC):
        for there in range(NY):
            source = columns_of(there, lax.rem(c + other, NC), EARLY, LATE)
            pairs.append((grad_hbm.at[:, source], late_ref.at[other, :, there * LATE:(there + 1) * LATE]))
    loads = [pltpu.make_async_copy(a, b, in_sem.at[i]) for i, (a, b) in enumerate(pairs)]
    for copy in loads:
        copy.start()
    loads[0].wait()
    loads[1].wait()
    live = live_ref[zh * 4 + x, (y * NZ + z) * NC + c]
    rank = jnp.where(zh == 0, z, NZ - 1 - z)
    keep = lax.broadcasted_iota(jnp.int32, (128, rows), 1) < live
    pairs = [
        (near_ref.at[0], up_hbm.at[:, width:]),
        (near_ref.at[1], down_hbm.at[:, width:]),
        (late_ref.at[1], swap_hbm.at[:, width:]),
        (late_ref.at[0], late_hbm),
    ]
    pairs += [(turned_ref, out.at[:, :width]) for out in (up_hbm, down_hbm, swap_hbm, own_hbm)]
    stores = [pltpu.make_async_copy(a, b, out_sem.at[i]) for i, (a, b) in enumerate(pairs)]
    for own in range(2):
        half = zh if own else 1 - zh
        for step in range(NZ):
            part = lax.rem(rank + 2 * NZ - 1 - step, NZ)
            block = (half * NZ + part) * 128
            cols = hidden_ref[:, pl.ds(pl.multiple_of(block, 128), 128)]
            turned = jnp.where(keep, cols.astype(f32).T, 0.0).astype(bf16)
            at = own * NZ + step
            down, across = slice(at % 2 * 128, (at % 2 + 1) * 128), at // 2 * rows
            turned_ref[down, across:across + rows] = turned
        if own == 0:
            for copy in loads[2:]:
                copy.wait()
            for copy in stores[:4]:
                copy.start()
    for copy in stores[4:]:
        copy.start()
    for copy in stores:
        copy.wait()


def prepare(live_tokens, hidden, grad):
    rows, width = hidden.shape
    early, late = NC * EARLY, NY * LATE
    widths = [width, width + early, width + early, width + late, late]
    return pl.pallas_call(
        prepare_kernel,
        out_shape=[jax.ShapeDtypeStruct((rows, cols), bf16) for cols in widths],
        in_specs=[HBM] * 3,
        out_specs=[HBM] * 5,
        scratch_shapes=[
            pltpu.SMEM(live_tokens.shape, live_tokens.dtype),
            pltpu.VMEM(hidden.shape, bf16),
            pltpu.VMEM(hidden.shape, bf16),
            pltpu.VMEM((2, rows, early), bf16),
            pltpu.VMEM((NC, rows, late), bf16),
            pltpu.SemaphoreType.DMA((2 + 2 * NC + NC * NY,)),
            pltpu.SemaphoreType.DMA((8,)),
        ],
        compiler_params=FULL,
        name="prepare",
    )(live_tokens, hidden, grad)


def pack_kernel(grad_hbm, after_ref, far_hbm, own_hbm, buffer, in_sem, out_sem):
    y, c = lax.axis_index("y"), lax.axis_index("c")
    pairs = []
    for i, dy in enumerate((2, 0)):
        for other in range(NC):
            source = columns_of(lax.rem(y + dy, NY), lax.rem(c + other, NC), 0, EARLY)
            pairs.append((grad_hbm.at[:, source], buffer.at[i, :, other * EARLY:(other + 1) * EARLY]))
    run([pltpu.make_async_copy(a, b, in_sem.at[i]) for i, (a, b) in enumerate(pairs)])
    pairs = [(buffer.at[0], far_hbm), (buffer.at[1], own_hbm)]
    run([pltpu.make_async_copy(a, b, out_sem.at[i]) for i, (a, b) in enumerate(pairs)])


def pack(grad, after):
    shape = (grad.shape[0], NC * EARLY)
    return pl.pallas_call(
        pack_kernel,
        out_shape=[jax.ShapeDtypeStruct(shape, bf16)] * 2,
        in_specs=[HBM] * 2,
        out_specs=[HBM] * 2,
        scratch_shapes=[
            pltpu.VMEM((2,) + shape, bf16),
            pltpu.SemaphoreType.DMA((2 * NC,)),
            pltpu.SemaphoreType.DMA((2,)),
        ],
        compiler_params=FULL,
        name="pack",
    )(grad, after)


def forward_kernel(up_ref, down_ref, after_ref, far_up_ref, far_down_ref, sem):
    half = far_up_ref.shape[1]
    pairs = [(up_ref.at[:, :half], far_up_ref), (down_ref.at[:, half:2 * half], far_down_ref)]
    run([pltpu.make_async_copy(a, b, sem.at[i]) for i, (a, b) in enumerate(pairs)])


def forward(up, down, half, after):
    return pl.pallas_call(
        forward_kernel,
        out_shape=[jax.ShapeDtypeStruct((up.shape[0], half), bf16)] * 2,
        in_specs=[ANY] * 3,
        out_specs=[VMEM] * 2,
        scratch_shapes=[pltpu.SemaphoreType.DMA((2,))],
        compiler_params=SMALL,
        name="forward",
    )(up, down, after)


def chip_product_kernel(own_ref, late_ref, swap_ref, *rest):
    outs, (left, right, sem) = rest[:2 * NZ], rest[2 * NZ:]
    rows, width = own_ref.shape
    pairs = [
        (own_ref, left.at[0]),
        (swap_ref.at[:, :width], left.at[1]),
        (late_ref, right.at[:rows, :]),
        (swap_ref.at[:, width:], right.at[rows:, :]),
    ]
    run([pltpu.make_async_copy(a, b, sem.at[i]) for i, (a, b) in enumerate(pairs)])
    for block in range(NZ):
        at = slice(block * rows, (block + 1) * rows)
        both = jnp.concatenate([left[0, :, at], left[1, :, at]], 1)
        total = jnp.dot(both, right[...], preferred_element_type=f32).astype(bf16)
        for i in range(2):
            outs[block * 2 + i][...] = total[i * 128:(i + 1) * 128]


def chip_product(own, late, swap):
    rows, width = own.shape
    cols = late.shape[1]
    return pl.pallas_call(
        chip_product_kernel,
        out_shape=[jax.ShapeDtypeStruct((128, cols), bf16)] * (2 * NZ),
        in_specs=[ANY] * 3,
        out_specs=[VMEM] * (2 * NZ),
        scratch_shapes=[
            pltpu.VMEM((NC, rows, width), bf16),
            pltpu.VMEM((NC * rows, cols), bf16),
            pltpu.SemaphoreType.DMA((4,)),
        ],
        compiler_params=PARAMS,
        name="chip_product",
    )(own, late, swap)


def split_kernel(*refs):
    y = lax.axis_index("y")
    for half in range(2):
        part_ref, moved_ref = refs[2 * half], refs[2 * half + 1]
        for dy, out_ref in enumerate(refs[4:]):
            at = pl.ds(pl.multiple_of(lax.rem(y + dy, NY) * LATE, 128), LATE)
            total = part_ref[:, at].astype(f32) + moved_ref[:, at].astype(f32)
            out_ref[half * 128:(half + 1) * 128, :] = total.astype(bf16)


def split(*terms):
    return pl.pallas_call(
        split_kernel,
        out_shape=[jax.ShapeDtypeStruct((256, LATE), bf16)] * NY,
        in_specs=[VMEM] * 4,
        out_specs=[VMEM] * NY,
        compiler_params=SMALL,
        name="split",
    )(*terms)


def product_kernel(part, n_after, *refs):
    hidden, grads = refs[:NY + 1], refs[NY + 1:2 * NY + 1]
    refs = refs[2 * NY + 1 + n_after:]
    outs, other_ref, (left, right, sem) = refs[:NZ], refs[NZ], refs[NZ + 1:]
    depth, width = hidden[0].shape
    rows, lead = outs[0].shape[0], part * width // 2
    pairs = []
    for dy in range(NY):
        if dy == 2:
            piece = hidden[NY] if part else hidden[2]
        else:
            piece = hidden[dy].at[:, lead:lead + width // 2]
        pairs.append((piece, left.at[dy]))
        first = grads[dy].shape[1] - NC * EARLY
        pairs.append((grads[dy].at[:, first:], right.at[dy * depth:(dy + 1) * depth, :]))
    run([pltpu.make_async_copy(a, b, sem.at[i]) for i, (a, b) in enumerate(pairs)])
    for pair in range(NZ // 2):
        at = slice(pair * depth, (pair + 1) * depth)
        block = jnp.concatenate([left[i, :, at] for i in range(NY)], 1)
        total = jnp.dot(block, right[...], preferred_element_type=f32)
        for i in range(2):
            outs[pair * 2 + i][...] = total[i * rows:(i + 1) * rows, :EARLY].astype(bf16)
        other_ref[pair * 2 * rows:(pair + 1) * 2 * rows, :] = total[:, EARLY:].astype(bf16)


def product(part, hidden, grads, after):
    tokens, width = hidden[0].shape
    depth, rows = NY * tokens, width // 2 // NZ
    shapes = [jax.ShapeDtypeStruct((rows, EARLY), bf16)] * NZ
    shapes.append(jax.ShapeDtypeStruct((rows * NZ, EARLY), bf16))
    return pl.pallas_call(
        functools.partial(product_kernel, part, len(after)),
        out_shape=shapes,
        in_specs=[ANY] * (2 * NY + 1 + len(after)),
        out_specs=[VMEM] * len(shapes),
        scratch_shapes=[
            pltpu.VMEM((NY, tokens, width // 2), bf16),
            pltpu.VMEM((depth, NC * EARLY), bf16),
            pltpu.SemaphoreType.DMA((2 * NY,)),
        ],
        compiler_params=PARAMS,
        cost_estimate=pl.CostEstimate(
            flops=COST * width * NC * EARLY * depth,
            bytes_accessed=width * (depth + NC * EARLY) + 2 * depth * NC * EARLY,
            transcendentals=0,
        ),
        name="product",
    )(*hidden, *grads, *after)


def add_kernel(terms, pieces, *refs):
    out_ref, rows = refs[-1], refs[-1].shape[0]
    total = None
    for ref, at in zip(refs, terms):
        term = ref[at:at + rows, :].astype(f32)
        total = term if total is None else total + term
    out_ref[:, :total.shape[1]] = total.astype(out_ref.dtype)
    if pieces is not None:
        total = None
        for ref in refs[len(terms):len(terms) + NY]:
            term = ref[pieces:pieces + rows, :].astype(f32)
            total = term if total is None else total + term
        out_ref[:, out_ref.shape[1] - total.shape[1]:] = total.astype(out_ref.dtype)


def add(terms, dtype, after=(), late=(), at=None, rows=128):
    cols = terms[0][0].shape[1] + (late[0].shape[1] if late else 0)
    return pl.pallas_call(
        functools.partial(add_kernel, tuple(first for _, first in terms), at),
        out_shape=jax.ShapeDtypeStruct((rows, cols), dtype),
        in_specs=[VMEM] * (len(terms) + len(late)) + [ANY] * len(after),
        out_specs=VMEM,
        compiler_params=SMALL,
        name="add",
    )(*[value for value, _ in terms], *late, *after)


def adamw_kernel(*refs):
    counts_ref, owned_refs = refs[0], refs[1:1 + NY]
    master_ref, first_ref, second_ref, new_master_ref, new_first_ref, new_second_ref = refs[1 + NY:]
    zh, x = lax.axis_index("zh"), lax.axis_index("x")
    y, z, c = lax.axis_index("y"), lax.axis_index("z"), lax.axis_index("c")
    held = counts_ref[zh * 4 + x, (y * NZ + z) * NC + c]
    slots, cols = master_ref.shape[0], COLS
    valid = lax.broadcasted_iota(jnp.int32, (slots, cols), 0) < held * BLK
    for dy in range(NY):
        for other in range(NC):
            at = columns_of(lax.rem(y + NY - dy, NY), lax.rem(c + other, NC))
            owned = owned_refs[dy][other].astype(f32)
            param = master_ref[:, at]
            first = beta_first * first_ref[:, at].astype(f32) + (1.0 - beta_first) * owned
            second = beta_second * second_ref[:, at].astype(f32) + (1.0 - beta_second) * owned * owned
            direction = first / bias_first / (jnp.sqrt(second / bias_second) + adam_eps)
            updated = param - learn_rate * (direction + weight_decay * param)
            new_master_ref[:, at] = jnp.where(valid, updated, 0.0)
            new_first_ref[:, at] = jnp.where(valid, first, 0.0).astype(bf16)
            new_second_ref[:, at] = jnp.where(valid, second, 0.0).astype(bf16)


def adamw(block_count, owned, master, moment1, moment2):
    shapes = [jax.ShapeDtypeStruct(a.shape, a.dtype) for a in (master, moment1, moment2)]
    return pl.pallas_call(
        adamw_kernel,
        out_shape=shapes,
        in_specs=[SMEM] + [VMEM] * (len(owned) + 3),
        out_specs=[VMEM] * 3,
        compiler_params=PARAMS,
        name="adamw",
    )(block_count, *owned, master, moment1, moment2)


def slot_choice(block_count, hblk, cap):
    y, z, c = lax.axis_index("y"), lax.axis_index("z"), lax.axis_index("c")
    counts = block_count[lax.axis_index("zh") * 4 + lax.axis_index("x")]
    owners = []
    for dy, dc in OFFSETS:
        owners.append(((y + dy) % NY * NZ + z) * NC + (c ^ dc))
    owners = jnp.stack(owners)
    before = jnp.arange(counts.shape[0], dtype=jnp.int32)[None, :] < owners[:, None]
    starts = jnp.sum(jnp.where(before, counts[None, :], 0), axis=1)
    slot = jnp.arange(cap, dtype=jnp.int32)
    block = jnp.minimum(starts[:, None] + slot[None, :], hblk - 1)
    per = hblk // NZ
    chunk = block // per
    rank = jnp.where(lax.axis_index("zh") == 0, z, NZ - 1 - z)
    chunk = (rank + NZ - chunk) % NZ
    place = chunk * per + block % per
    rows = place[:, :, None] * BLK + jnp.arange(BLK, dtype=jnp.int32)
    rows = rows.reshape(-1)
    return (rows[:, None] == jnp.arange(hblk * BLK, dtype=jnp.int32)[None, :]).astype(bf16)


def per_device(hidden_act, grad_out, live_tokens, block_count, master, moment1, moment2):
    half = hidden_act.shape[1] // 2
    slots = master.shape[1]
    own, up, down, swap, late = prepare(live_tokens, hidden_act, grad_out)
    choice = slot_choice(block_count, half // BLK, slots // BLK)
    near = [send_group(up, 1, 0), send_group(down, 3, 0)]
    opposite, mine = pack(grad_out, own)
    grads = [mine, near[0], send_group(opposite, 2, 0), near[1]]

    parts = chip_product(own, late, send_group(swap, 0, 1))
    moving, steps = [parts[0], parts[NZ]], []
    for step in range(1, NZ - 1):
        moving = [
            add([(parts[half * NZ + step], 0), (send_ring(moving[half], 1), 0)], bf16)
            for half in range(2)
        ]
        steps.append(moving[1])
    pieces = split(
        parts[NZ - 1], send_ring(moving[0], 1), parts[2 * NZ - 1], send_ring(moving[1], 1)
    )
    late = [send_group(piece, dy, 0) for dy, piece in enumerate(pieces)]

    far = forward(near[0], near[1], half, steps[FORWARD])
    far = [send_group(far[0], 1, 0), send_group(far[1], 3, 0)]
    hidden = [own, near[0], far[0], near[1], far[1]]
    sums, after = [], [pieces[0]]
    for part in range(2):
        parts = product(part, hidden, grads, [] if part else after)
        sibling = send_group(parts[NZ], 0, 1)
        moved = []
        for step in range(NZ):
            terms = [(parts[step], 0), (sibling, step * 128)] + moved
            if step < NZ - 1:
                total = add(terms, bf16, after if part and not step else ())
                moved = [(send_ring(total, 1), 0)]
            else:
                total = add(terms, f32 if part else bf16, (), late, part * 128)
            if step == LAG:
                after = [total]
        sums.append(total)
    tile = (sums[1] + send_mirror(sums[0]).astype(f32)).astype(bf16)
    gathered = jnp.concatenate([tile] + [send_ring(tile, d) for d in range(1, NZ)], 0)
    picked = jnp.dot(choice, gathered, preferred_element_type=f32).astype(bf16)
    picked = picked.reshape(NY, NC, slots, COLS)
    both = jnp.stack([picked[:, 0], send_group(picked[:, 1], 0, 1)], 1)
    owned = [send_group(both[dy], dy, 0) for dy in range(NY)]
    outs = adamw(block_count, owned, master[0], moment1[0], moment2[0])
    return tuple(out[None] for out in outs)


def solution(mesh):
    fine = Mesh(mesh.devices.reshape(2, 4, NY, NZ, NC), ("zh", "x", "y", "z", "c"))
    pipe, edp = ("zh", "x"), ("y", "z", "c")
    shard = P(pipe, edp, None)
    tokens = P(pipe + edp, None)
    return jax.shard_map(
        per_device,
        mesh=fine,
        in_specs=(tokens, tokens, P(), P(), shard, shard, shard),
        out_specs=(shard, shard, shard),
        check_vma=False,
    )
```

```python
import functools
import jax
import jax.numpy as jnp
from jax import lax
from jax.experimental import pallas as pl
from jax.experimental.pallas import tpu as pltpu
from jax.sharding import Mesh, PartitionSpec as P

BLK = 8
NY, NZ, NC = 4, 4, 2
NEAR = (1, NY - 1)
COLS, LATE = 896, 256
EARLY = COLS - LATE
LAG, FORWARD = 0, 1
COST = 1
OFFSETS = tuple((dy, dc) for dy in range(NY) for dc in range(NC))

beta_first = 0.9
beta_second = 0.95
learn_rate = 0.00022
weight_decay = 0.1
adam_eps = 1e-08
bias_first = 1.0 - 0.9**20
bias_second = 1.0 - 0.95**20

bf16 = jnp.bfloat16
f32 = jnp.float32
VMEM = pl.BlockSpec(memory_space=pltpu.VMEM)
SMEM = pl.BlockSpec(memory_space=pltpu.SMEM)
ANY = pl.BlockSpec(memory_space=pl.ANY)
HBM = pl.BlockSpec(memory_space=pltpu.HBM)
PARAMS = pltpu.CompilerParams(vmem_limit_bytes=40 * 1024 * 1024)
SMALL = pltpu.CompilerParams(vmem_limit_bytes=8 * 1024 * 1024)
FULL = pltpu.CompilerParams(vmem_limit_bytes=62 * 1024 * 1024)


def send_group(value, dy, dc):
    if dy == 0 and dc == 0:
        return value
    pairs = []
    for y in range(NY):
        for c in range(NC):
            pairs.append((y * NC + c, (y + dy) % NY * NC + (c ^ dc)))
    return lax.ppermute(value, ("y", "c"), pairs)


def send_ring(value, steps):
    pairs = []
    for z in range(NZ):
        pairs.append((z, (z + steps) % NZ))
        pairs.append((NZ + z, NZ + (z + NZ - steps) % NZ))
    return lax.ppermute(value, ("zh", "z"), pairs)


def gather(tile):
    half = tile.shape[0] // 2
    up, down = send_ring(tile, 1), send_ring(tile, NZ - 1)
    far = jnp.concatenate([send_ring(up[:half], 1), send_ring(down[half:], NZ - 1)], 0)
    return jnp.concatenate([tile, up, far, down], 0)


def send_mirror(value):
    pairs = []
    for zh in range(2):
        for x in range(4):
            for z in range(NZ):
                source = (zh * 4 + x) * NZ + z
                target = ((1 - zh) * 4 + 3 - x) * NZ + NZ - 1 - z
                pairs.append((source, target))
    return lax.ppermute(value, ("zh", "x", "z"), pairs)


def columns_of(y, c, base=0, cols=COLS):
    return pl.ds(pl.multiple_of((y * NC + c) * COLS + base, 128), cols)


def run(copies):
    for copy in copies:
        copy.start()
    for copy in copies:
        copy.wait()


def prepare_kernel(live_hbm, hidden_hbm, grad_hbm, own_hbm, up_hbm, down_hbm, swap_hbm, late_hbm, *rest):
    live_ref, hidden_ref, turned_ref, near_ref, late_ref, in_sem, out_sem = rest
    zh, x = lax.axis_index("zh"), lax.axis_index("x")
    y, z, c = lax.axis_index("y"), lax.axis_index("z"), lax.axis_index("c")
    rows, width = hidden_ref.shape
    pairs = [(hidden_hbm, hidden_ref), (live_hbm, live_ref)]
    for i, dy in enumerate(NEAR):
        for other in range(NC):
            source = columns_of(lax.rem(y + dy, NY), lax.rem(c + other, NC), 0, EARLY)
            pairs.append((grad_hbm.at[:, source], near_ref.at[i, :, other * EARLY:(other + 1) * EARLY]))
    for other in range(NC):
        for there in range(NY):
            source = columns_of(there, lax.rem(c + other, NC), EARLY, LATE)
            pairs.append((grad_hbm.at[:, source], late_ref.at[other, :, there * LATE:(there + 1) * LATE]))
    loads = [pltpu.make_async_copy(a, b, in_sem.at[i]) for i, (a, b) in enumerate(pairs)]
    for copy in loads:
        copy.start()
    loads[0].wait()
    loads[1].wait()
    live = live_ref[zh * 4 + x, (y * NZ + z) * NC + c]
    rank = jnp.where(zh == 0, z, NZ - 1 - z)
    keep = lax.broadcasted_iota(jnp.int32, (128, rows), 1) < live
    pairs = [
        (near_ref.at[0], up_hbm.at[:, width:]),
        (near_ref.at[1], down_hbm.at[:, width:]),
        (late_ref.at[1], swap_hbm.at[:, width:]),
        (late_ref.at[0], late_hbm),
    ]
    pairs += [(turned_ref, out.at[:, :width]) for out in (up_hbm, down_hbm, swap_hbm, own_hbm)]
    stores = [pltpu.make_async_copy(a, b, out_sem.at[i]) for i, (a, b) in enumerate(pairs)]
    for own in range(2):
        half = zh if own else 1 - zh
        for step in range(NZ):
            part = lax.rem(rank + 2 * NZ - 1 - step, NZ)
            block = (half * NZ + part) * 128
            cols = hidden_ref[:, pl.ds(pl.multiple_of(block, 128), 128)]
            turned = jnp.where(keep, cols.astype(f32).T, 0.0).astype(bf16)
            at = own * NZ + step
            down, across = slice(at % 2 * 128, (at % 2 + 1) * 128), at // 2 * rows
            turned_ref[down, across:across + rows] = turned
        if own == 0:
            for copy in loads[2:]:
                copy.wait()
            for copy in stores[:4]:
                copy.start()
    for copy in stores[4:]:
        copy.start()
    for copy in stores:
        copy.wait()


def prepare(live_tokens, hidden, grad):
    rows, width = hidden.shape
    early, late = NC * EARLY, NY * LATE
    widths = [width, width + early, width + early, width + late, late]
    return pl.pallas_call(
        prepare_kernel,
        out_shape=[jax.ShapeDtypeStruct((rows, cols), bf16) for cols in widths],
        in_specs=[HBM] * 3,
        out_specs=[HBM] * 5,
        scratch_shapes=[
            pltpu.SMEM(live_tokens.shape, live_tokens.dtype),
            pltpu.VMEM(hidden.shape, bf16),
            pltpu.VMEM(hidden.shape, bf16),
            pltpu.VMEM((2, rows, early), bf16),
            pltpu.VMEM((NC, rows, late), bf16),
            pltpu.SemaphoreType.DMA((2 + 2 * NC + NC * NY,)),
            pltpu.SemaphoreType.DMA((8,)),
        ],
        compiler_params=FULL,
        name="prepare",
    )(live_tokens, hidden, grad)


def pack_kernel(grad_hbm, after_ref, far_hbm, own_hbm, buffer, in_sem, out_sem):
    y, c = lax.axis_index("y"), lax.axis_index("c")
    pairs = []
    for i, dy in enumerate((2, 0)):
        for other in range(NC):
            source = columns_of(lax.rem(y + dy, NY), lax.rem(c + other, NC), 0, EARLY)
            pairs.append((grad_hbm.at[:, source], buffer.at[i, :, other * EARLY:(other + 1) * EARLY]))
    run([pltpu.make_async_copy(a, b, in_sem.at[i]) for i, (a, b) in enumerate(pairs)])
    pairs = [(buffer.at[0], far_hbm), (buffer.at[1], own_hbm)]
    run([pltpu.make_async_copy(a, b, out_sem.at[i]) for i, (a, b) in enumerate(pairs)])


def pack(grad, after):
    shape = (grad.shape[0], NC * EARLY)
    return pl.pallas_call(
        pack_kernel,
        out_shape=[jax.ShapeDtypeStruct(shape, bf16)] * 2,
        in_specs=[HBM] * 2,
        out_specs=[HBM] * 2,
        scratch_shapes=[
            pltpu.VMEM((2,) + shape, bf16),
            pltpu.SemaphoreType.DMA((2 * NC,)),
            pltpu.SemaphoreType.DMA((2,)),
        ],
        compiler_params=FULL,
        name="pack",
    )(grad, after)


def forward_kernel(up_ref, down_ref, after_ref, far_up_ref, far_down_ref, sem):
    half = far_up_ref.shape[1]
    pairs = [(up_ref.at[:, :half], far_up_ref), (down_ref.at[:, half:2 * half], far_down_ref)]
    run([pltpu.make_async_copy(a, b, sem.at[i]) for i, (a, b) in enumerate(pairs)])


def forward(up, down, half, after):
    return pl.pallas_call(
        forward_kernel,
        out_shape=[jax.ShapeDtypeStruct((up.shape[0], half), bf16)] * 2,
        in_specs=[ANY] * 3,
        out_specs=[VMEM] * 2,
        scratch_shapes=[pltpu.SemaphoreType.DMA((2,))],
        compiler_params=SMALL,
        name="forward",
    )(up, down, after)


def chip_product_kernel(own_ref, late_ref, swap_ref, *rest):
    outs, (left, right, sem) = rest[:2 * NZ], rest[2 * NZ:]
    rows, width = own_ref.shape
    pairs = [
        (own_ref, left.at[0]),
        (swap_ref.at[:, :width], left.at[1]),
        (late_ref, right.at[:rows, :]),
        (swap_ref.at[:, width:], right.at[rows:, :]),
    ]
    run([pltpu.make_async_copy(a, b, sem.at[i]) for i, (a, b) in enumerate(pairs)])
    for block in range(NZ):
        at = slice(block * rows, (block + 1) * rows)
        both = jnp.concatenate([left[0, :, at], left[1, :, at]], 1)
        total = jnp.dot(both, right[...], preferred_element_type=f32).astype(bf16)
        for i in range(2):
            outs[block * 2 + i][...] = total[i * 128:(i + 1) * 128]


def chip_product(own, late, swap):
    rows, width = own.shape
    cols = late.shape[1]
    return pl.pallas_call(
        chip_product_kernel,
        out_shape=[jax.ShapeDtypeStruct((128, cols), bf16)] * (2 * NZ),
        in_specs=[ANY] * 3,
        out_specs=[VMEM] * (2 * NZ),
        scratch_shapes=[
            pltpu.VMEM((NC, rows, width), bf16),
            pltpu.VMEM((NC * rows, cols), bf16),
            pltpu.SemaphoreType.DMA((4,)),
        ],
        compiler_params=PARAMS,
        name="chip_product",
    )(own, late, swap)


def split_kernel(*refs):
    y = lax.axis_index("y")
    for half in range(2):
        part_ref, moved_ref = refs[2 * half], refs[2 * half + 1]
        for dy, out_ref in enumerate(refs[4:]):
            at = pl.ds(pl.multiple_of(lax.rem(y + dy, NY) * LATE, 128), LATE)
            total = part_ref[:, at].astype(f32) + moved_ref[:, at].astype(f32)
            out_ref[half * 128:(half + 1) * 128, :] = total.astype(bf16)


def split(*terms):
    return pl.pallas_call(
        split_kernel,
        out_shape=[jax.ShapeDtypeStruct((256, LATE), bf16)] * NY,
        in_specs=[VMEM] * 4,
        out_specs=[VMEM] * NY,
        compiler_params=SMALL,
        name="split",
    )(*terms)


def product_kernel(part, n_after, *refs):
    hidden, grads = refs[:NY + 1], refs[NY + 1:2 * NY + 1]
    refs = refs[2 * NY + 1 + n_after:]
    outs, other_ref, (left, right, sem) = refs[:NZ], refs[NZ], refs[NZ + 1:]
    depth, width = hidden[0].shape
    rows, lead = outs[0].shape[0], part * width // 2
    first, second = [], []
    for dy in range(NY):
        if dy == 2:
            piece = hidden[NY] if part else hidden[2]
        else:
            piece = hidden[dy].at[:, lead:lead + width // 2]
        first.append((piece, left.at[dy]))
        start = grads[dy].shape[1] - NC * EARLY
        rows_of = right.at[dy * depth:(dy + 1) * depth]
        first.append((grads[dy].at[:, start + EARLY:], rows_of.at[:, EARLY:]))
        second.append((grads[dy].at[:, start:start + EARLY], rows_of.at[:, :EARLY]))
    copies = [pltpu.make_async_copy(a, b, sem.at[i]) for i, (a, b) in enumerate(first + second)]
    for copy in copies:
        copy.start()
    for copy in copies[:2 * NY]:
        copy.wait()
    blocks = []
    for pair in range(NZ // 2):
        at = slice(pair * depth, (pair + 1) * depth)
        blocks.append(jnp.concatenate([left[i, :, at] for i in range(NY)], 1))
        total = jnp.dot(blocks[pair], right[:, EARLY:], preferred_element_type=f32)
        other_ref[pair * 2 * rows:(pair + 1) * 2 * rows, :] = total.astype(bf16)
    for copy in copies[2 * NY:]:
        copy.wait()
    for pair in range(NZ // 2):
        total = jnp.dot(blocks[pair], right[:, :EARLY], preferred_element_type=f32)
        for i in range(2):
            outs[pair * 2 + i][...] = total[i * rows:(i + 1) * rows].astype(bf16)


def product(part, hidden, grads, after):
    tokens, width = hidden[0].shape
    depth, rows = NY * tokens, width // 2 // NZ
    shapes = [jax.ShapeDtypeStruct((rows, EARLY), bf16)] * NZ
    shapes.append(jax.ShapeDtypeStruct((rows * NZ, EARLY), bf16))
    return pl.pallas_call(
        functools.partial(product_kernel, part, len(after)),
        out_shape=shapes,
        in_specs=[ANY] * (2 * NY + 1 + len(after)),
        out_specs=[VMEM] * len(shapes),
        scratch_shapes=[
            pltpu.VMEM((NY, tokens, width // 2), bf16),
            pltpu.VMEM((depth, NC * EARLY), bf16),
            pltpu.SemaphoreType.DMA((3 * NY,)),
        ],
        compiler_params=PARAMS,
        cost_estimate=pl.CostEstimate(
            flops=COST * width * NC * EARLY * depth,
            bytes_accessed=width * (depth + NC * EARLY) + 2 * depth * NC * EARLY,
            transcendentals=0,
        ),
        name="product",
    )(*hidden, *grads, *after)


def add_kernel(terms, pieces, *refs):
    out_ref, rows = refs[-1], refs[-1].shape[0]
    total = None
    for ref, at in zip(refs, terms):
        term = ref[at:at + rows, :].astype(f32)
        total = term if total is None else total + term
    out_ref[:, :total.shape[1]] = total.astype(out_ref.dtype)
    if pieces is not None:
        total = None
        for ref in refs[len(terms):len(terms) + NY]:
            term = ref[pieces:pieces + rows, :].astype(f32)
            total = term if total is None else total + term
        out_ref[:, out_ref.shape[1] - total.shape[1]:] = total.astype(out_ref.dtype)


def add(terms, dtype, after=(), late=(), at=None, rows=128):
    cols = terms[0][0].shape[1] + (late[0].shape[1] if late else 0)
    return pl.pallas_call(
        functools.partial(add_kernel, tuple(first for _, first in terms), at),
        out_shape=jax.ShapeDtypeStruct((rows, cols), dtype),
        in_specs=[VMEM] * (len(terms) + len(late)) + [ANY] * len(after),
        out_specs=VMEM,
        compiler_params=SMALL,
        name="add",
    )(*[value for value, _ in terms], *late, *after)


def adamw_kernel(*refs):
    counts_ref, owned_refs = refs[0], refs[1:1 + NY]
    master_ref, first_ref, second_ref, new_master_ref, new_first_ref, new_second_ref = refs[1 + NY:]
    zh, x = lax.axis_index("zh"), lax.axis_index("x")
    y, z, c = lax.axis_index("y"), lax.axis_index("z"), lax.axis_index("c")
    held = counts_ref[zh * 4 + x, (y * NZ + z) * NC + c]
    slots, cols = master_ref.shape[0], COLS
    valid = lax.broadcasted_iota(jnp.int32, (slots, cols), 0) < held * BLK
    for dy in range(NY):
        for other in range(NC):
            at = columns_of(lax.rem(y + NY - dy, NY), lax.rem(c + other, NC))
            owned = owned_refs[dy][other].astype(f32)
            param = master_ref[:, at]
            first = beta_first * first_ref[:, at].astype(f32) + (1.0 - beta_first) * owned
            second = beta_second * second_ref[:, at].astype(f32) + (1.0 - beta_second) * owned * owned
            direction = first / bias_first / (jnp.sqrt(second / bias_second) + adam_eps)
            updated = param - learn_rate * (direction + weight_decay * param)
            new_master_ref[:, at] = jnp.where(valid, updated, 0.0)
            new_first_ref[:, at] = jnp.where(valid, first, 0.0).astype(bf16)
            new_second_ref[:, at] = jnp.where(valid, second, 0.0).astype(bf16)


def adamw(block_count, owned, master, moment1, moment2):
    shapes = [jax.ShapeDtypeStruct(a.shape, a.dtype) for a in (master, moment1, moment2)]
    return pl.pallas_call(
        adamw_kernel,
        out_shape=shapes,
        in_specs=[SMEM] + [VMEM] * (len(owned) + 3),
        out_specs=[VMEM] * 3,
        compiler_params=PARAMS,
        name="adamw",
    )(block_count, *owned, master, moment1, moment2)


def slot_choice(block_count, hblk, cap):
    y, z, c = lax.axis_index("y"), lax.axis_index("z"), lax.axis_index("c")
    counts = block_count[lax.axis_index("zh") * 4 + lax.axis_index("x")]
    owners = []
    for dy, dc in OFFSETS:
        owners.append(((y + dy) % NY * NZ + z) * NC + (c ^ dc))
    owners = jnp.stack(owners)
    before = jnp.arange(counts.shape[0], dtype=jnp.int32)[None, :] < owners[:, None]
    starts = jnp.sum(jnp.where(before, counts[None, :], 0), axis=1)
    slot = jnp.arange(cap, dtype=jnp.int32)
    block = jnp.minimum(starts[:, None] + slot[None, :], hblk - 1)
    per = hblk // NZ
    chunk = block // per
    rank = jnp.where(lax.axis_index("zh") == 0, z, NZ - 1 - z)
    chunk = (rank + NZ - chunk) % NZ
    place = chunk * per + block % per
    rows = place[:, :, None] * BLK + jnp.arange(BLK, dtype=jnp.int32)
    rows = rows.reshape(-1)
    return (rows[:, None] == jnp.arange(hblk * BLK, dtype=jnp.int32)[None, :]).astype(bf16)


def per_device(hidden_act, grad_out, live_tokens, block_count, master, moment1, moment2):
    half = hidden_act.shape[1] // 2
    slots = master.shape[1]
    own, up, down, swap, late = prepare(live_tokens, hidden_act, grad_out)
    choice = slot_choice(block_count, half // BLK, slots // BLK)
    near = [send_group(up, 1, 0), send_group(down, 3, 0)]
    opposite, mine = pack(grad_out, own)
    grads = [mine, near[0], send_group(opposite, 2, 0), near[1]]

    parts = chip_product(own, late, send_group(swap, 0, 1))
    moving, steps = [parts[0], parts[NZ]], []
    for step in range(1, NZ - 1):
        moving = [
            add([(parts[half * NZ + step], 0), (send_ring(moving[half], 1), 0)], bf16)
            for half in range(2)
        ]
        steps.append(moving[1])
    pieces = split(
        parts[NZ - 1], send_ring(moving[0], 1), parts[2 * NZ - 1], send_ring(moving[1], 1)
    )
    late = [send_group(piece, dy, 0) for dy, piece in enumerate(pieces)]

    far = forward(near[0], near[1], half, steps[FORWARD])
    far = [send_group(far[0], 1, 0), send_group(far[1], 3, 0)]
    hidden = [own, near[0], far[0], near[1], far[1]]
    sums, after = [], [pieces[0]]
    for part in range(2):
        parts = product(part, hidden, grads, [] if part else after)
        sibling = send_group(parts[NZ], 0, 1)
        moved = []
        for step in range(NZ):
            terms = [(parts[step], 0), (sibling, step * 128)] + moved
            if step < NZ - 1:
                total = add(terms, bf16)
                moved = [(send_ring(total, 1), 0)]
            else:
                total = add(terms, f32 if part else bf16, (), late, part * 128)
            if step == LAG:
                after = [total]
        sums.append(total)
    tile = (sums[1] + send_mirror(sums[0]).astype(f32)).astype(bf16)
    gathered = gather(tile)
    picked = jnp.dot(choice, gathered, preferred_element_type=f32).astype(bf16)
    picked = picked.reshape(NY, NC, slots, COLS)
    both = jnp.stack([picked[:, 0], send_group(picked[:, 1], 0, 1)], 1)
    owned = [send_group(both[dy], dy, 0) for dy in range(NY)]
    outs = adamw(block_count, owned, master[0], moment1[0], moment2[0])
    return tuple(out[None] for out in outs)


def solution(mesh):
    fine = Mesh(mesh.devices.reshape(2, 4, NY, NZ, NC), ("zh", "x", "y", "z", "c"))
    pipe, edp = ("zh", "x"), ("y", "z", "c")
    shard = P(pipe, edp, None)
    tokens = P(pipe + edp, None)
    return jax.shard_map(
        per_device,
        mesh=fine,
        in_specs=(tokens, tokens, P(), P(), shard, shard, shard),
        out_specs=(shard, shard, shard),
        check_vma=False,
    )
```

```python
import functools
import jax
import jax.numpy as jnp
from jax import lax
from jax.experimental import pallas as pl
from jax.experimental.pallas import tpu as pltpu
from jax.sharding import Mesh, PartitionSpec as P

BLK = 8
NY, NZ, NC = 4, 4, 2
NEAR = (1, NY - 1)
COLS, LATE = 896, 256
EARLY = COLS - LATE
LAG, FORWARD = 0, 1
COST = 1
OFFSETS = tuple((dy, dc) for dy in range(NY) for dc in range(NC))

beta_first = 0.9
beta_second = 0.95
learn_rate = 0.00022
weight_decay = 0.1
adam_eps = 1e-08
bias_first = 1.0 - 0.9**20
bias_second = 1.0 - 0.95**20

bf16 = jnp.bfloat16
f32 = jnp.float32
VMEM = pl.BlockSpec(memory_space=pltpu.VMEM)
SMEM = pl.BlockSpec(memory_space=pltpu.SMEM)
ANY = pl.BlockSpec(memory_space=pl.ANY)
HBM = pl.BlockSpec(memory_space=pltpu.HBM)
PARAMS = pltpu.CompilerParams(vmem_limit_bytes=40 * 1024 * 1024)
SMALL = pltpu.CompilerParams(vmem_limit_bytes=8 * 1024 * 1024)
FULL = pltpu.CompilerParams(vmem_limit_bytes=62 * 1024 * 1024)


def send_group(value, dy, dc):
    if dy == 0 and dc == 0:
        return value
    pairs = []
    for y in range(NY):
        for c in range(NC):
            pairs.append((y * NC + c, (y + dy) % NY * NC + (c ^ dc)))
    return lax.ppermute(value, ("y", "c"), pairs)


def send_ring(value, steps):
    pairs = []
    for z in range(NZ):
        pairs.append((z, (z + steps) % NZ))
        pairs.append((NZ + z, NZ + (z + NZ - steps) % NZ))
    return lax.ppermute(value, ("zh", "z"), pairs)


def gather(tile):
    half = tile.shape[0] // 2
    up, down = send_ring(tile, 1), send_ring(tile, NZ - 1)
    far = jnp.concatenate([send_ring(up[:half], 1), send_ring(down[half:], NZ - 1)], 0)
    return jnp.concatenate([tile, up, far, down], 0)


def send_mirror(value):
    pairs = []
    for zh in range(2):
        for x in range(4):
            for z in range(NZ):
                source = (zh * 4 + x) * NZ + z
                target = ((1 - zh) * 4 + 3 - x) * NZ + NZ - 1 - z
                pairs.append((source, target))
    return lax.ppermute(value, ("zh", "x", "z"), pairs)


def columns_of(y, c, base=0, cols=COLS):
    return pl.ds(pl.multiple_of((y * NC + c) * COLS + base, 128), cols)


def run(copies):
    for copy in copies:
        copy.start()
    for copy in copies:
        copy.wait()


def prepare_kernel(live_hbm, hidden_hbm, grad_hbm, own_hbm, up_hbm, down_hbm, swap_hbm, late_hbm, *rest):
    live_ref, hidden_ref, turned_ref, near_ref, late_ref, in_sem, out_sem = rest
    zh, x = lax.axis_index("zh"), lax.axis_index("x")
    y, z, c = lax.axis_index("y"), lax.axis_index("z"), lax.axis_index("c")
    rows, width = hidden_ref.shape
    pairs = [(hidden_hbm, hidden_ref), (live_hbm, live_ref)]
    for i, dy in enumerate(NEAR):
        for other in range(NC):
            source = columns_of(lax.rem(y + dy, NY), lax.rem(c + other, NC), 0, EARLY)
            pairs.append((grad_hbm.at[:, source], near_ref.at[i, :, other * EARLY:(other + 1) * EARLY]))
    for other in range(NC):
        for there in range(NY):
            source = columns_of(there, lax.rem(c + other, NC), EARLY, LATE)
            pairs.append((grad_hbm.at[:, source], late_ref.at[other, :, there * LATE:(there + 1) * LATE]))
    loads = [pltpu.make_async_copy(a, b, in_sem.at[i]) for i, (a, b) in enumerate(pairs)]
    for copy in loads:
        copy.start()
    loads[0].wait()
    loads[1].wait()
    live = live_ref[zh * 4 + x, (y * NZ + z) * NC + c]
    rank = jnp.where(zh == 0, z, NZ - 1 - z)
    keep = lax.broadcasted_iota(jnp.int32, (128, rows), 1) < live
    pairs = [
        (near_ref.at[0], up_hbm.at[:, width:]),
        (near_ref.at[1], down_hbm.at[:, width:]),
        (late_ref.at[1], swap_hbm.at[:, width:]),
        (late_ref.at[0], late_hbm),
    ]
    pairs += [(turned_ref, out.at[:, :width]) for out in (up_hbm, down_hbm, swap_hbm, own_hbm)]
    stores = [pltpu.make_async_copy(a, b, out_sem.at[i]) for i, (a, b) in enumerate(pairs)]
    for own in range(2):
        half = zh if own else 1 - zh
        for step in range(NZ):
            part = lax.rem(rank + 2 * NZ - 1 - step, NZ)
            block = (half * NZ + part) * 128
            cols = hidden_ref[:, pl.ds(pl.multiple_of(block, 128), 128)]
            turned = jnp.where(keep, cols.astype(f32).T, 0.0).astype(bf16)
            at = own * NZ + step
            down, across = slice(at % 2 * 128, (at % 2 + 1) * 128), at // 2 * rows
            turned_ref[down, across:across + rows] = turned
        if own == 0:
            for copy in loads[2:]:
                copy.wait()
            for copy in stores[:4]:
                copy.start()
    for copy in stores[4:]:
        copy.start()
    for copy in stores:
        copy.wait()


def prepare(live_tokens, hidden, grad):
    rows, width = hidden.shape
    early, late = NC * EARLY, NY * LATE
    widths = [width, width + early, width + early, width + late, late]
    return pl.pallas_call(
        prepare_kernel,
        out_shape=[jax.ShapeDtypeStruct((rows, cols), bf16) for cols in widths],
        in_specs=[HBM] * 3,
        out_specs=[HBM] * 5,
        scratch_shapes=[
            pltpu.SMEM(live_tokens.shape, live_tokens.dtype),
            pltpu.VMEM(hidden.shape, bf16),
            pltpu.VMEM(hidden.shape, bf16),
            pltpu.VMEM((2, rows, early), bf16),
            pltpu.VMEM((NC, rows, late), bf16),
            pltpu.SemaphoreType.DMA((2 + 2 * NC + NC * NY,)),
            pltpu.SemaphoreType.DMA((8,)),
        ],
        compiler_params=FULL,
        name="prepare",
    )(live_tokens, hidden, grad)


def pack_kernel(grad_hbm, after_ref, far_hbm, own_hbm, buffer, in_sem, out_sem):
    y, c = lax.axis_index("y"), lax.axis_index("c")
    pairs = []
    for i, dy in enumerate((2, 0)):
        for other in range(NC):
            source = columns_of(lax.rem(y + dy, NY), lax.rem(c + other, NC), 0, EARLY)
            pairs.append((grad_hbm.at[:, source], buffer.at[i, :, other * EARLY:(other + 1) * EARLY]))
    run([pltpu.make_async_copy(a, b, in_sem.at[i]) for i, (a, b) in enumerate(pairs)])
    pairs = [(buffer.at[0], far_hbm), (buffer.at[1], own_hbm)]
    run([pltpu.make_async_copy(a, b, out_sem.at[i]) for i, (a, b) in enumerate(pairs)])


def pack(grad, after):
    shape = (grad.shape[0], NC * EARLY)
    return pl.pallas_call(
        pack_kernel,
        out_shape=[jax.ShapeDtypeStruct(shape, bf16)] * 2,
        in_specs=[HBM] * 2,
        out_specs=[HBM] * 2,
        scratch_shapes=[
            pltpu.VMEM((2,) + shape, bf16),
            pltpu.SemaphoreType.DMA((2 * NC,)),
            pltpu.SemaphoreType.DMA((2,)),
        ],
        compiler_params=FULL,
        name="pack",
    )(grad, after)


def forward_kernel(up_ref, down_ref, after_ref, far_up_ref, far_down_ref, sem):
    half = far_up_ref.shape[1]
    pairs = [(up_ref.at[:, :half], far_up_ref), (down_ref.at[:, half:2 * half], far_down_ref)]
    run([pltpu.make_async_copy(a, b, sem.at[i]) for i, (a, b) in enumerate(pairs)])


def forward(up, down, half, after):
    return pl.pallas_call(
        forward_kernel,
        out_shape=[jax.ShapeDtypeStruct((up.shape[0], half), bf16)] * 2,
        in_specs=[ANY] * 3,
        out_specs=[VMEM] * 2,
        scratch_shapes=[pltpu.SemaphoreType.DMA((2,))],
        compiler_params=SMALL,
        name="forward",
    )(up, down, after)


def chip_product_kernel(own_ref, late_ref, swap_ref, *rest):
    outs, (left, right, sem) = rest[:2 * NZ], rest[2 * NZ:]
    rows, width = own_ref.shape
    pairs = [
        (own_ref, left.at[0]),
        (swap_ref.at[:, :width], left.at[1]),
        (late_ref, right.at[:rows, :]),
        (swap_ref.at[:, width:], right.at[rows:, :]),
    ]
    run([pltpu.make_async_copy(a, b, sem.at[i]) for i, (a, b) in enumerate(pairs)])
    for block in range(NZ):
        at = slice(block * rows, (block + 1) * rows)
        both = jnp.concatenate([left[0, :, at], left[1, :, at]], 1)
        total = jnp.dot(both, right[...], preferred_element_type=f32).astype(bf16)
        for i in range(2):
            outs[block * 2 + i][...] = total[i * 128:(i + 1) * 128]


def chip_product(own, late, swap):
    rows, width = own.shape
    cols = late.shape[1]
    return pl.pallas_call(
        chip_product_kernel,
        out_shape=[jax.ShapeDtypeStruct((128, cols), bf16)] * (2 * NZ),
        in_specs=[ANY] * 3,
        out_specs=[VMEM] * (2 * NZ),
        scratch_shapes=[
            pltpu.VMEM((NC, rows, width), bf16),
            pltpu.VMEM((NC * rows, cols), bf16),
            pltpu.SemaphoreType.DMA((4,)),
        ],
        compiler_params=PARAMS,
        name="chip_product",
    )(own, late, swap)


def split_kernel(*refs):
    y = lax.axis_index("y")
    for half in range(2):
        part_ref, moved_ref = refs[2 * half], refs[2 * half + 1]
        for dy, out_ref in enumerate(refs[4:]):
            at = pl.ds(pl.multiple_of(lax.rem(y + dy, NY) * LATE, 128), LATE)
            total = part_ref[:, at].astype(f32) + moved_ref[:, at].astype(f32)
            out_ref[half * 128:(half + 1) * 128, :] = total.astype(bf16)


def split(*terms):
    return pl.pallas_call(
        split_kernel,
        out_shape=[jax.ShapeDtypeStruct((256, LATE), bf16)] * NY,
        in_specs=[VMEM] * 4,
        out_specs=[VMEM] * NY,
        compiler_params=SMALL,
        name="split",
    )(*terms)


def product_kernel(part, n_after, *refs):
    hidden, grads = refs[:NY + 1], refs[NY + 1:2 * NY + 1]
    refs = refs[2 * NY + 1 + n_after:]
    outs, other_ref, (left, right, sem) = refs[:NZ], refs[NZ], refs[NZ + 1:]
    depth, width = hidden[0].shape
    rows, lead = outs[0].shape[0], part * width // 2
    first, second = [], []
    for dy in range(NY):
        if dy == 2:
            piece = hidden[NY] if part else hidden[2]
        else:
            piece = hidden[dy].at[:, lead:lead + width // 2]
        first.append((piece, left.at[dy]))
        start = grads[dy].shape[1] - NC * EARLY
        rows_of = right.at[dy * depth:(dy + 1) * depth]
        first.append((grads[dy].at[:, start + EARLY:], rows_of.at[:, EARLY:]))
        second.append((grads[dy].at[:, start:start + EARLY], rows_of.at[:, :EARLY]))
    copies = [pltpu.make_async_copy(a, b, sem.at[i]) for i, (a, b) in enumerate(first + second)]
    for copy in copies:
        copy.start()
    for copy in copies[:2 * NY]:
        copy.wait()
    blocks = []
    for pair in range(NZ // 2):
        at = slice(pair * depth, (pair + 1) * depth)
        blocks.append(jnp.concatenate([left[i, :, at] for i in range(NY)], 1))
        total = jnp.dot(blocks[pair], right[:, EARLY:], preferred_element_type=f32)
        other_ref[pair * 2 * rows:(pair + 1) * 2 * rows, :] = total.astype(bf16)
    for copy in copies[2 * NY:]:
        copy.wait()
    for pair in range(NZ // 2):
        total = jnp.dot(blocks[pair], right[:, :EARLY], preferred_element_type=f32)
        for i in range(2):
            outs[pair * 2 + i][...] = total[i * rows:(i + 1) * rows].astype(bf16)


def product(part, hidden, grads, after):
    tokens, width = hidden[0].shape
    depth, rows = NY * tokens, width // 2 // NZ
    shapes = [jax.ShapeDtypeStruct((rows, EARLY), bf16)] * NZ
    shapes.append(jax.ShapeDtypeStruct((rows * NZ, EARLY), bf16))
    return pl.pallas_call(
        functools.partial(product_kernel, part, len(after)),
        out_shape=shapes,
        in_specs=[ANY] * (2 * NY + 1 + len(after)),
        out_specs=[VMEM] * len(shapes),
        scratch_shapes=[
            pltpu.VMEM((NY, tokens, width // 2), bf16),
            pltpu.VMEM((depth, NC * EARLY), bf16),
            pltpu.SemaphoreType.DMA((3 * NY,)),
        ],
        compiler_params=PARAMS,
        cost_estimate=pl.CostEstimate(
            flops=COST * width * NC * EARLY * depth,
            bytes_accessed=width * (depth + NC * EARLY) + 2 * depth * NC * EARLY,
            transcendentals=0,
        ),
        name="product",
    )(*hidden, *grads, *after)


def add_kernel(terms, pieces, *refs):
    out_ref, rows = refs[-1], refs[-1].shape[0]
    total = None
    for ref, at in zip(refs, terms):
        term = ref[at:at + rows, :].astype(f32)
        total = term if total is None else total + term
    out_ref[:, :total.shape[1]] = total.astype(out_ref.dtype)
    if pieces is not None:
        total = None
        for ref in refs[len(terms):len(terms) + NY]:
            term = ref[pieces:pieces + rows, :].astype(f32)
            total = term if total is None else total + term
        out_ref[:, out_ref.shape[1] - total.shape[1]:] = total.astype(out_ref.dtype)


def add(terms, dtype, after=(), late=(), at=None, rows=128):
    cols = terms[0][0].shape[1] + (late[0].shape[1] if late else 0)
    return pl.pallas_call(
        functools.partial(add_kernel, tuple(first for _, first in terms), at),
        out_shape=jax.ShapeDtypeStruct((rows, cols), dtype),
        in_specs=[VMEM] * (len(terms) + len(late)) + [ANY] * len(after),
        out_specs=VMEM,
        compiler_params=SMALL,
        name="add",
    )(*[value for value, _ in terms], *late, *after)


def adamw_kernel(*refs):
    counts_ref, owned_refs = refs[0], refs[1:1 + NY]
    master_ref, first_ref, second_ref, new_master_ref, new_first_ref, new_second_ref = refs[1 + NY:]
    zh, x = lax.axis_index("zh"), lax.axis_index("x")
    y, z, c = lax.axis_index("y"), lax.axis_index("z"), lax.axis_index("c")
    held = counts_ref[zh * 4 + x, (y * NZ + z) * NC + c]
    slots, cols = master_ref.shape[0], COLS
    valid = lax.broadcasted_iota(jnp.int32, (slots, cols), 0) < held * BLK
    for dy in range(NY):
        for other in range(NC):
            at = columns_of(lax.rem(y + NY - dy, NY), lax.rem(c + other, NC))
            owned = owned_refs[dy][other].astype(f32)
            param = master_ref[:, at]
            first = beta_first * first_ref[:, at].astype(f32) + (1.0 - beta_first) * owned
            second = beta_second * second_ref[:, at].astype(f32) + (1.0 - beta_second) * owned * owned
            direction = first / bias_first / (jnp.sqrt(second / bias_second) + adam_eps)
            updated = param - learn_rate * (direction + weight_decay * param)
            new_master_ref[:, at] = jnp.where(valid, updated, 0.0)
            new_first_ref[:, at] = jnp.where(valid, first, 0.0).astype(bf16)
            new_second_ref[:, at] = jnp.where(valid, second, 0.0).astype(bf16)


def adamw(block_count, owned, master, moment1, moment2):
    shapes = [jax.ShapeDtypeStruct(a.shape, a.dtype) for a in (master, moment1, moment2)]
    return pl.pallas_call(
        adamw_kernel,
        out_shape=shapes,
        in_specs=[SMEM] + [VMEM] * (len(owned) + 3),
        out_specs=[VMEM] * 3,
        compiler_params=PARAMS,
        name="adamw",
    )(block_count, *owned, master, moment1, moment2)


def slot_choice(block_count, hblk, cap):
    y, z, c = lax.axis_index("y"), lax.axis_index("z"), lax.axis_index("c")
    counts = block_count[lax.axis_index("zh") * 4 + lax.axis_index("x")]
    owners = []
    for dy, dc in OFFSETS:
        owners.append(((y + dy) % NY * NZ + z) * NC + (c ^ dc))
    owners = jnp.stack(owners)
    before = jnp.arange(counts.shape[0], dtype=jnp.int32)[None, :] < owners[:, None]
    starts = jnp.sum(jnp.where(before, counts[None, :], 0), axis=1)
    slot = jnp.arange(cap, dtype=jnp.int32)
    block = jnp.minimum(starts[:, None] + slot[None, :], hblk - 1)
    per = hblk // NZ
    chunk = block // per
    rank = jnp.where(lax.axis_index("zh") == 0, z, NZ - 1 - z)
    chunk = (rank + NZ - chunk) % NZ
    place = chunk * per + block % per
    rows = place[:, :, None] * BLK + jnp.arange(BLK, dtype=jnp.int32)
    rows = rows.reshape(-1)
    return (rows[:, None] == jnp.arange(hblk * BLK, dtype=jnp.int32)[None, :]).astype(bf16)


def per_device(hidden_act, grad_out, live_tokens, block_count, master, moment1, moment2):
    half = hidden_act.shape[1] // 2
    slots = master.shape[1]
    own, up, down, swap, late = prepare(live_tokens, hidden_act, grad_out)
    choice = slot_choice(block_count, half // BLK, slots // BLK)
    near = [send_group(up, 1, 0), send_group(down, 3, 0)]
    opposite, mine = pack(grad_out, own)
    grads = [mine, near[0], send_group(opposite, 2, 0), near[1]]

    parts = chip_product(own, late, send_group(swap, 0, 1))
    moving, steps = [parts[0], parts[NZ]], []
    for step in range(1, NZ - 1):
        moving = [
            add([(parts[half * NZ + step], 0), (send_ring(moving[half], 1), 0)], bf16)
            for half in range(2)
        ]
        steps.append(moving[1])
    pieces = split(
        parts[NZ - 1], send_ring(moving[0], 1), parts[2 * NZ - 1], send_ring(moving[1], 1)
    )
    late = [send_group(piece, dy, 0) for dy, piece in enumerate(pieces)]

    far = forward(near[0], near[1], half, own)
    far = [send_group(far[0], 1, 0), send_group(far[1], 3, 0)]
    hidden = [own, near[0], far[0], near[1], far[1]]
    sums, after = [], [pieces[0]]
    for part in range(2):
        parts = product(part, hidden, grads, [] if part else after)
        sibling = send_group(parts[NZ], 0, 1)
        moved = []
        for step in range(NZ):
            terms = [(parts[step], 0), (sibling, step * 128)] + moved
            if step < NZ - 1:
                total = add(terms, bf16)
                moved = [(send_ring(total, 1), 0)]
            else:
                total = add(terms, f32 if part else bf16, (), late, part * 128)
            if step == LAG:
                after = [total]
        sums.append(total)
    tile = (sums[1] + send_mirror(sums[0]).astype(f32)).astype(bf16)
    gathered = gather(tile)
    picked = jnp.dot(choice, gathered, preferred_element_type=f32).astype(bf16)
    picked = picked.reshape(NY, NC, slots, COLS)
    both = jnp.stack([picked[:, 0], send_group(picked[:, 1], 0, 1)], 1)
    owned = [send_group(both[dy], dy, 0) for dy in range(NY)]
    outs = adamw(block_count, owned, master[0], moment1[0], moment2[0])
    return tuple(out[None] for out in outs)


def solution(mesh):
    fine = Mesh(mesh.devices.reshape(2, 4, NY, NZ, NC), ("zh", "x", "y", "z", "c"))
    pipe, edp = ("zh", "x"), ("y", "z", "c")
    shard = P(pipe, edp, None)
    tokens = P(pipe + edp, None)
    return jax.shard_map(
        per_device,
        mesh=fine,
        in_specs=(tokens, tokens, P(), P(), shard, shard, shard),
        out_specs=(shard, shard, shard),
        check_vma=False,
    )
```
